256 devices in a mesh: tm: 64 (over z, y, x_lo), space: 4 (over x_hi, core).
Axes of the slice: x: 4 (x_hi: 2, x_lo: 2; x = x_hi * 2 + x_lo), y: 4, z: 8, core: 2. Of those that a mesh axis runs over, the one named last changes fastest.
Arguments:
- qkv: bfloat16 [3, 256, 128, 4096], P(None, 'tm', 'space'), may hold values from -32 to 32
- clip_lengths: int32 [16], replicated, may hold values from 1 to 40, 256 in all
- wo: bfloat16 [4096, 4096], P(None, 'space'), may hold values from -0.09375 to 0.09375
Outputs:
- mixed: bfloat16 [256, 128, 4096], P('tm', 'space')
The draws below stay inside these ranges and needn't reach their ends.
Inputs may be any that keep to these rules, and one draw needn't show every extreme that they name: `clip_lengths`: the lengths sum to 256; the longest is exactly 40.
All inputs are finite; a program needn't handle non-finite values.
Results may differ from the reference program's by a relative error of at most 0.013.
Values may be sent and summed in bfloat16 or wider, within the bound.
No kernel may reach another device: no remote copies, remote signals or barrier semaphores. Data moves between devices by JAX's collectives and lax.ppermute only.
A program may use at most 128 MiB of HBM per device.

```python
import math
import jax
import jax.numpy as jnp
import numpy as np
from jax import lax

D = 4096
HEADS = 32
HS = 128
TOK = 128
FRAMES = 256
MAXCLIP = 40
CLIPS = 16


def draw_qkv(key, part):
    key = jax.random.fold_in(key, 7)
    return jnp.clip(jax.random.normal(key, (3, FRAMES, TOK, D)), -6.0, 6.0).astype(jnp.bfloat16)


def block_scale(own_key, extent, cuts, smallest, high):
    level = 1.0
    for dim, shards_of in cuts:
        draws = jax.random.uniform(jax.random.fold_in(jax.random.fold_in(own_key, 6), dim), (shards_of,), jnp.float32, smallest / len(cuts), high / len(cuts))
        level = level * jnp.repeat(jnp.exp(draws), extent[dim] // shards_of).reshape((-1,) + (1,) * (len(extent) - 1 - dim))
    return level


def length_profile(amount, total, bound, slope):
    portions = [(1 << 20) // math.isqrt(grade ** slope) + 1 for grade in range(2, amount + 1)]
    rest, holding = total - bound - (amount - 1), [1] * (amount - 1)
    while rest > 0:
        free = [i for i in range(amount - 1) if holding[i] < bound]
        pool, budget = sum([portions[i] for i in free]), rest
        for i in free:
            addition = min(bound - holding[i], max(1, budget * portions[i] // pool), rest)
            holding[i] = holding[i] + addition
            rest = rest - addition
    return np.array([bound] + holding)


def uneven(rng, amount, total, bound, slope):
    if amount == 2:
        one = jax.random.randint(rng, (), max(1, total - bound), min(bound, total - 1) + 1)
        return jnp.stack([one, total - one])
    sizes = jnp.asarray(length_profile(amount, total, bound, slope), jnp.int32)
    twos = (amount - 1) // 2
    donor, taker = sizes[1:1 + 2 * twos:2], sizes[2:2 + 2 * twos:2]
    slack = jnp.minimum(donor - 1, bound - taker)
    shifted = jax.random.randint(jax.random.fold_in(rng, 1), (twos,), 0, 1 << 20) % (slack + 1)
    sizes = sizes.at[1:1 + 2 * twos:2].set(donor - shifted).at[2:2 + 2 * twos:2].set(taker + shifted)
    return sizes[jax.random.permutation(jax.random.fold_in(rng, 2), amount)]


def noise(key, shape, width, reach, cuts=(), kind=jnp.bfloat16):
    values = width * jax.random.normal(key, shape, jnp.float32)
    if cuts:
        values = values * block_scale(key, shape, cuts, -0.22, 0.18)
    return jnp.clip(values, -reach, reach).astype(kind)


def setup_inputs(seed: int = 0) -> dict:
    keys = jax.random.split(jax.random.key(seed), 4)
    qkv = draw_qkv(jax.random.fold_in(keys[3], 71), 0)
    clip_lengths = uneven(keys[1], CLIPS, FRAMES, MAXCLIP, 2).astype(jnp.int32)
    wo = noise(keys[2], (D, D), D ** -0.5, 0.09375, ((1, 4),))
    return {"qkv": qkv, "clip_lengths": clip_lengths, "wo": wo}


def clip_ids(clip_lengths, frames):
    clip_ends = jnp.cumsum(clip_lengths)
    starts = clip_ends - clip_lengths
    return jnp.sum((starts[None, :] <= frames[:, None]).astype(jnp.int32), axis=1) - 1


def weights_of(scores, allowed):
    masked = jnp.where(allowed, scores, -1e30)
    top_score = jnp.max(masked, axis=-1, keepdims=True)
    raised = jnp.where(allowed, jnp.exp(masked - top_score), 0.0)
    return (raised / jnp.sum(raised, axis=-1, keepdims=True)).astype(jnp.bfloat16)


def reference(qkv, clip_lengths, wo):
    half_width = D // 2
    head_count = HEADS // 2
    score_scale = HS ** -0.5
    spatial = qkv[:, :, :, :half_width].reshape(3, FRAMES, TOK, head_count, HS)

    def spatial_frame(item_block):
        queries = item_block[0].astype(jnp.float32)
        key_rows = item_block[1].astype(jnp.float32)
        values = item_block[2].astype(jnp.float32)
        scores = jnp.einsum("thd,shd->hts", queries, key_rows) * score_scale
        allowed = jnp.ones((TOK,), dtype=bool)
        weights = weights_of(scores, allowed)
        return jnp.einsum("hts,shd->thd", weights.astype(jnp.float32), values).astype(jnp.bfloat16)

    spatial_out = lax.map(spatial_frame, jnp.moveaxis(spatial, 1, 0))
    temporal = qkv[:, :, :, half_width:].reshape(3, FRAMES, TOK, head_count, HS)
    all_frames = jnp.arange(FRAMES, dtype=jnp.int32)
    clip_index = clip_ids(clip_lengths, all_frames)
    allowed = (clip_index[None, :] == clip_index[:, None]) & (all_frames[None, :] <= all_frames[:, None])

    def temporal_token(item_block):
        queries = item_block[0].astype(jnp.float32)
        key_rows = item_block[1].astype(jnp.float32)
        values = item_block[2].astype(jnp.float32)
        scores = jnp.einsum("fhd,ghd->hfg", queries, key_rows) * score_scale
        weights = weights_of(scores, allowed[None])
        return jnp.einsum("hfg,ghd->fhd", weights.astype(jnp.float32), values).astype(jnp.bfloat16)

    temporal_out = lax.map(temporal_token, jnp.moveaxis(temporal, 2, 0))
    temporal_out = jnp.moveaxis(temporal_out, 0, 1)
    attention = jnp.concatenate(
        [spatial_out.reshape(FRAMES, TOK, half_width), temporal_out.reshape(FRAMES, TOK, half_width)], axis=-1
    ).reshape(FRAMES * TOK, D)
    projected = jnp.dot(attention, wo, preferred_element_type=jnp.float32).astype(jnp.bfloat16)
    return projected.reshape(FRAMES, TOK, D)
```

```python
import jax
import jax.numpy as jnp
import numpy as np
from jax import lax
from jax.experimental import pallas as pl
from jax.experimental.pallas import tpu as pltpu
from jax.sharding import Mesh, PartitionSpec as P

HS = 128
Z, Y, XL, XH, C = 8, 4, 2, 2, 2
PLANE = Y * XL
SWAP = [(0, 1), (1, 0)]
SCALE = HS ** (-0.5)
VMEM = 56 * 1024 * 1024
F32 = jnp.float32
BF16 = jnp.bfloat16
GROUP = 8


def softmax_parts(scores):
    top = jnp.max(scores, axis=-1, keepdims=True)
    raised = jnp.exp(scores - top)
    return raised.astype(BF16), jnp.sum(raised, axis=-1, keepdims=True)


def spatial_kernel(heads, place, own, queries_far, keyvals_far, mate_own, mate_far, out):
    for head in range(heads):
        cols = slice(head * HS, (head + 1) * HS)
        queries = jnp.concatenate([own[0, 0, :, cols], queries_far[0, :, cols]], axis=0)
        key_rows = jnp.concatenate(
            [own[1, 0, :, cols], keyvals_far[0, 0, :, cols], mate_own[0, 0, :, cols], mate_far[0, 0, :, cols]], axis=0
        )
        values = jnp.concatenate(
            [own[2, 0, :, cols], keyvals_far[1, 0, :, cols], mate_own[1, 0, :, cols], mate_far[1, 0, :, cols]], axis=0
        )
        scores = lax.dot_general(queries, key_rows, (((1,), (1,)), ((), ())), preferred_element_type=F32) * SCALE
        raised, total = softmax_parts(scores)
        result = (jnp.dot(raised, values, preferred_element_type=F32) / total).astype(BF16)
        rows = result.shape[0] // 2
        out[0, 0, :, cols] = result[:rows]
        out[1, 0, :, cols] = result[rows:]


def spatial_attend(place, qkv, queries_far, keyvals_far, mate_own, mate_far):
    _, frames, tok, width = keyvals_far.shape
    heads = width // HS

    def body(*refs):
        spatial_kernel(heads, *refs)

    pair = pl.BlockSpec((2, 1, tok, width), lambda f, place: (0, f, 0, 0))
    return pl.pallas_call(
        body,
        grid_spec=pltpu.PrefetchScalarGridSpec(
            num_scalar_prefetch=1,
            grid=(frames,),
            in_specs=[
                pl.BlockSpec((3, 1, tok, width), lambda f, place: (0, f, 0, place[1])),
                pl.BlockSpec((1, tok, width), lambda f, place: (f, 0, 0)),
                pair,
                pair,
                pair,
            ],
            out_specs=pair,
        ),
        out_shape=jax.ShapeDtypeStruct((2, frames, tok, width), BF16),
        compiler_params=pltpu.CompilerParams(vmem_limit_bytes=VMEM),
        name="spatial",
    )(place, qkv, queries_far, keyvals_far, mate_own, mate_far)


def temporal_kernel(clips, place, lengths, queries, own, before, before2, out, bias):
    sources, _, groups, rows, _ = queries.shape
    frames_dev = rows // GROUP
    query_rows = sources * rows
    past_frames = (sources + before2.shape[0]) * frames_dev
    key_count = query_rows + past_frames * GROUP

    @pl.when(pl.program_id(0) == 0)
    def _():
        row = lax.broadcasted_iota(jnp.int32, (query_rows, 1), 0)
        first = place[0] * (sources * frames_dev)
        frame = first + row // GROUP
        start = jnp.zeros_like(frame)
        begin = jnp.int32(0)
        for clip in range(clips):
            start = jnp.where(frame >= begin, begin, start)
            begin = begin + lengths[clip]
        token = (row % GROUP) * 4096
        low = token + start - first + past_frames
        high = token + frame - first + past_frames
        col = lax.broadcasted_iota(jnp.int32, (1, key_count), 1)
        code = (col % GROUP) * 4096 + col // GROUP
        bias[...] = jnp.where((code >= low) & (code <= high), 0.0, -1e30)

    pieces = []
    for group in range(groups):
        def rows_of(ref, which):
            return ref[:, which, 0, group].reshape(-1, HS)

        key_rows = jnp.concatenate([rows_of(before2, 0), rows_of(before, 0), rows_of(own, 0)], axis=0)
        values = jnp.concatenate([rows_of(before2, 1), rows_of(before, 1), rows_of(own, 1)], axis=0)
        scores = lax.dot_general(
            queries[:, 0, group].reshape(-1, HS), key_rows, (((1,), (1,)), ((), ())), preferred_element_type=F32
        )
        raised, total = softmax_parts(scores * SCALE + bias[...])
        result = jnp.dot(raised, values, preferred_element_type=F32) / total
        pieces.append(result.reshape(sources * frames_dev, 1, GROUP, HS))
    joined = jnp.concatenate(pieces, axis=1).reshape(sources, frames_dev * groups * GROUP, HS)
    out[...] = joined.astype(BF16)


def temporal_attend(place, lengths, queries, own, before, before2):
    sources, heads, groups, rows, _ = queries.shape
    clips = lengths.shape[0]
    tok_rows = groups * rows

    def body(*refs):
        temporal_kernel(clips, *refs)

    def keyvals_spec(count):
        return pl.BlockSpec((count, 2, 1, groups, rows, HS), lambda h, place, lengths: (0, 0, h, 0, 0, 0))

    key_count = (2 * sources + before2.shape[0]) * rows
    return pl.pallas_call(
        body,
        grid_spec=pltpu.PrefetchScalarGridSpec(
            num_scalar_prefetch=2,
            grid=(heads,),
            in_specs=[
                pl.BlockSpec((sources, 1, groups, rows, HS), lambda h, place, lengths: (0, h, 0, 0, 0)),
                keyvals_spec(sources),
                keyvals_spec(sources),
                keyvals_spec(before2.shape[0]),
            ],
            out_specs=pl.BlockSpec((sources, tok_rows, HS), lambda h, place, lengths: (0, 0, h)),
            scratch_shapes=[pltpu.VMEM((sources * rows, key_count), F32)],
        ),
        out_shape=jax.ShapeDtypeStruct((sources, tok_rows, heads * HS), BF16),
        compiler_params=pltpu.CompilerParams(vmem_limit_bytes=VMEM),
        name="temporal",
    )(place, lengths, queries, own, before, before2)


def project_spatial(place, near, far, wo, wo_mate):
    _, rows, width = near.shape
    cols = wo.shape[1]
    block = 512
    per = width // block

    def body(place, near, far, wo, wo_mate, out):
        step = pl.program_id(0)

        def add(first, own_rows, far_rows):
            for weights, side in ((wo, 0), (wo_mate, 1)):
                for which, lhs in ((0, own_rows), (1, far_rows)):
                    part = jnp.dot(lhs, weights[...], preferred_element_type=F32)
                    out[which, :, side] = part if first else out[which, :, side] + part

        @pl.when(step == 0)
        def _():
            add(True, near[0], near[1])

        @pl.when((step > 0) & (step < per))
        def _():
            add(False, near[0], near[1])

        @pl.when(step >= per)
        def _():
            add(False, far[1], far[0])

    weights = pl.BlockSpec(
        (block, cols), lambda k, place: (jnp.where(k < per, place[1] * per + k, (1 - place[1]) * per + k - per), 0)
    )
    return pl.pallas_call(
        body,
        grid_spec=pltpu.PrefetchScalarGridSpec(
            num_scalar_prefetch=1,
            grid=(2 * per,),
            in_specs=[
                pl.BlockSpec((2, rows, block), lambda k, place: (0, 0, jnp.minimum(k, per - 1))),
                pl.BlockSpec((2, rows, block), lambda k, place: (0, 0, jnp.maximum(k - per, 0))),
                weights,
                weights,
            ],
            out_specs=pl.BlockSpec((2, rows, 2, cols), lambda k, place: (0, 0, 0, 0)),
        ),
        out_shape=jax.ShapeDtypeStruct((2, rows, 2, cols), F32),
        compiler_params=pltpu.CompilerParams(vmem_limit_bytes=VMEM),
        name="project_spatial",
    )(place, near, far, wo, wo_mate)


def project_temporal(place, which, partial, returned, wo, wo_mate):
    _, rows, _, cols = partial.shape
    sources, _, _, width = returned.shape
    per = 2
    block = per * width
    steps = sources // per
    skip = wo.shape[0] // block - steps

    def body(place, partial, returned, wo, wo_mate, out, total):
        step = pl.program_id(0)
        lhs = jnp.concatenate([returned[i, 0] for i in range(per)], axis=1)

        @pl.when(step == 0)
        def _():
            total[...] = partial[0]

        for weights, side in ((wo, 0), (wo_mate, 1)):
            total[:, side] = total[:, side] + jnp.dot(lhs, weights[...], preferred_element_type=F32)

        @pl.when(step == steps - 1)
        def _():
            out[...] = total[...].astype(BF16)

    weights = pl.BlockSpec((block, cols), lambda k, place: (skip + k, 0))
    return pl.pallas_call(
        body,
        grid_spec=pltpu.PrefetchScalarGridSpec(
            num_scalar_prefetch=1,
            grid=(steps,),
            in_specs=[
                pl.BlockSpec((1, rows, 2, cols), lambda k, place: (which, 0, 0, 0)),
                pl.BlockSpec(
                    (per, 1, rows, width),
                    lambda k, place: (k, (1 - place[1]) if which else place[1], 0, 0),
                ),
                weights,
                weights,
            ],
            out_specs=pl.BlockSpec((rows, 2, cols), lambda k, place: (0, 0, 0)),
            scratch_shapes=[pltpu.VMEM((rows, 2, cols), F32)],
        ),
        out_shape=jax.ShapeDtypeStruct((rows, 2, cols), BF16),
        compiler_params=pltpu.CompilerParams(vmem_limit_bytes=VMEM),
        name="project_far" if which else "project_own",
    )(place, partial, returned, wo, wo_mate)


def on_device(qkv, clip_lengths, wo):
    _, frames, tok, model_width = qkv.shape
    half = model_width // 2
    quarter = half // 2
    z_place = lax.axis_index("z")
    x_place = lax.axis_index("xh")
    c_place = lax.axis_index("c")
    place = jnp.stack([z_place, x_place]).astype(jnp.int32)

    heads = half // HS // PLANE
    groups = tok // GROUP
    rows = frames * GROUP

    def by_plane(block):
        count = block.shape[0]
        split = block.reshape(count, frames, groups, GROUP, PLANE, heads, HS)
        return split.transpose(4, 0, 5, 2, 1, 3, 6).reshape(PLANE, count, heads, groups, rows, HS)

    keyvals = lax.all_to_all(by_plane(qkv[1:, :, :, half:]), ("y", "xl"), 0, 0, tiled=True)
    queries = lax.all_to_all(by_plane(qkv[:1, :, :, half:]), ("y", "xl"), 0, 0, tiled=True)[:, 0]
    before = lax.ppermute(keyvals, "z", [(i, (i + 1) % Z) for i in range(Z)])
    before2 = lax.ppermute(keyvals[PLANE - 2 :], "z", [(i, (i + 2) % Z) for i in range(Z)])

    own_cols = x_place * quarter
    far_cols = (1 - x_place) * quarter
    keyvals_far = lax.ppermute(
        lax.dynamic_slice(qkv, (1, 0, 0, far_cols), (2, frames, tok, quarter)), "xh", SWAP
    )
    queries_far = lax.ppermute(
        lax.dynamic_slice(qkv, (0, 0, 0, far_cols), (1, frames, tok, quarter)), "xh", SWAP
    )[0]
    mate_own = lax.ppermute(
        lax.dynamic_slice(qkv, (1, 0, 0, own_cols), (2, frames, tok, quarter)), "c", SWAP
    )
    mate_far = lax.ppermute(keyvals_far, "c", SWAP)
    wo_mate = lax.ppermute(wo, "c", SWAP)

    near = spatial_attend(place, qkv, queries_far, keyvals_far, mate_own, mate_far)
    near = near.reshape(2, frames * tok, quarter)
    far = lax.ppermute(near, "xh", SWAP)
    partial = project_spatial(place, near, far, wo, wo_mate)

    temporal = temporal_attend(place, clip_lengths, queries, keyvals, before, before2)
    sent = jnp.broadcast_to(temporal[:, None], (PLANE, XH) + temporal.shape[1:])
    sent = sent.reshape((PLANE * XH,) + temporal.shape[1:])
    returned = lax.all_to_all(sent, ("y", "xl", "xh"), 0, 0, tiled=True)
    returned = returned.reshape((PLANE, XH) + temporal.shape[1:])

    cols = wo.shape[1]
    for_partner = project_temporal(place, 1, partial, returned, wo, wo_mate)
    arrived = lax.ppermute(for_partner, "xh", SWAP)
    own = project_temporal(place, 0, partial, returned, wo, wo_mate)
    mixed = jnp.zeros((frames * tok, model_width), BF16)
    for block, place_x in ((own, x_place), (arrived, 1 - x_place)):
        mixed = lax.dynamic_update_slice(mixed, block[:, 0], (0, (place_x * C + c_place) * cols))
        mixed = lax.dynamic_update_slice(mixed, block[:, 1], (0, (place_x * C + 1 - c_place) * cols))
    return mixed.reshape(frames, tok, model_width)


def solution(mesh):
    fine = Mesh(mesh.devices.reshape(Z, Y, XL, XH, C), ("z", "y", "xl", "xh", "c"))
    return jax.shard_map(
        on_device,
        mesh=fine,
        in_specs=(P(None, ("z", "y", "xl"), ("xh", "c"), None), P(), P(None, ("xh", "c"))),
        out_specs=P(("z", "y", "xl"), ("xh", "c"), None),
        check_vma=False,
    )
```

```python
import jax
import jax.numpy as jnp
import numpy as np
from jax import lax
from jax.experimental import pallas as pl
from jax.experimental.pallas import tpu as pltpu
from jax.sharding import Mesh, PartitionSpec as P

HS = 128
Z, Y, XL, XH, C = 8, 4, 2, 2, 2
PLANE = Y * XL
EXP2_SCALE = HS ** (-0.5) * float(np.log2(np.e))
F32 = jnp.float32
BF16 = jnp.bfloat16
GROUP = 8
ROUNDS = 2

SWAP = [(0, 1), (1, 0)]

SMEM = pl.BlockSpec(memory_space=pltpu.SMEM)
WHOLE = pl.BlockSpec(memory_space=pltpu.VMEM)
ANYWHERE = pl.BlockSpec(memory_space=pl.ANY)
IN_HBM = pl.BlockSpec(memory_space=pltpu.HBM)
WIDE = 60
QUICK = pl.CostEstimate(flops=1024, bytes_accessed=1024, transcendentals=0)


def kernel_params(mebibytes):
    return pltpu.CompilerParams(vmem_limit_bytes=mebibytes * 1024 * 1024)


def softmax_parts(scores):
    top = jnp.max(scores, axis=-1, keepdims=True)
    return jnp.exp2((scores - top) * EXP2_SCALE).astype(BF16)


def weighted(raised, values):
    both = jnp.concatenate([values, jnp.ones_like(values)], axis=1)
    result = jnp.dot(raised, both, preferred_element_type=F32)
    return result[:, :HS] / result[:, HS:]


def spatial_attend(own, far, mate_own, mate_far, after):
    _, frames, tok, width = own.shape

    def body(own, far, mate_own, mate_far, after, out):
        blocks = [(f, slice(head * HS, (head + 1) * HS)) for f in range(frames) for head in range(width // HS)]

        def keyvals_of(which, f, cols):
            return jnp.concatenate([ref[which, f, :, cols] for ref in (own, far, mate_own, mate_far)], axis=0)

        for first in range(0, len(blocks), 8):
            batch = blocks[first : first + 8]
            scores = []
            for f, cols in batch:
                queries = jnp.concatenate([own[0, f, :, cols], far[0, f, :, cols]], axis=0)
                scores.append(
                    lax.dot_general(
                        queries, keyvals_of(1, f, cols), (((1,), (1,)), ((), ())), preferred_element_type=F32
                    )
                )
            raised = [softmax_parts(block) for block in scores]
            results = [weighted(block, keyvals_of(2, f, cols)).astype(BF16) for block, (f, cols) in zip(raised, batch)]
            for result, (f, cols) in zip(results, batch):
                out[0, f, :, cols] = result[:tok]
                out[1, f, :, cols] = result[tok:]

    return pl.pallas_call(
        body,
        in_specs=[WHOLE] * 4 + [ANYWHERE],
        out_specs=WHOLE,
        out_shape=jax.ShapeDtypeStruct((2, frames, tok, width), BF16),
        compiler_params=kernel_params(16),
        cost_estimate=QUICK,
        name="spatial",
    )(own, far, mate_own, mate_far, after)


def temporal_kernel(clips, turn, place, lengths, queries, own, before, before2, after, out, bias):
    sources, _, groups, rows, _ = queries.shape
    frames_dev = rows // GROUP
    query_rows = sources * rows
    past_frames = (sources + before2.shape[1]) * frames_dev
    key_count = query_rows + past_frames * GROUP

    row = lax.broadcasted_iota(jnp.int32, (query_rows, 1), 0)
    first = place[0] * (sources * frames_dev)
    frame = first + row // GROUP
    start = jnp.zeros_like(frame)
    begin = jnp.int32(0)
    for clip in range(clips):
        start = jnp.where(frame >= begin, begin, start)
        begin = begin + lengths[clip]
    token = (row % GROUP) * 4096
    low = token + start - first + past_frames
    high = token + frame - first + past_frames
    col = lax.broadcasted_iota(jnp.int32, (1, key_count), 1)
    code = (col % GROUP) * 4096 + col // GROUP
    bias[...] = jnp.where((code >= low) & (code <= high), 0.0, -1e30)

    pieces = []
    for group in range(groups):
        def rows_of(ref, which):
            return ref[:, which, group].reshape(-1, HS)

        key_rows = jnp.concatenate([rows_of(before2.at[turn], 0), rows_of(before, 0), rows_of(own, 0)], axis=0)
        values = jnp.concatenate([rows_of(before2.at[turn], 1), rows_of(before, 1), rows_of(own, 1)], axis=0)
        scores = lax.dot_general(
            queries[:, turn, group].reshape(-1, HS), key_rows, (((1,), (1,)), ((), ())), preferred_element_type=F32
        )
        result = weighted(softmax_parts(scores + bias[...]), values)
        pieces.append(result.reshape(sources * frames_dev, 1, GROUP, HS))
    joined = jnp.concatenate(pieces, axis=1).reshape(sources, frames_dev * groups * GROUP, HS).astype(BF16)
    for copy in range(XH):
        out[:, copy] = joined


def temporal_attend(turn, place, lengths, queries, own, before, before2, after):
    sources, _, groups, rows, _ = queries.shape
    clips = lengths.shape[0]

    def body(*refs):
        temporal_kernel(clips, turn, *refs)

    key_count = (2 * sources + before2.shape[1]) * rows
    return pl.pallas_call(
        body,
        in_specs=[SMEM, SMEM, WHOLE, WHOLE, WHOLE, WHOLE, ANYWHERE],
        out_specs=WHOLE,
        out_shape=jax.ShapeDtypeStruct((sources, XH, groups * rows, HS), BF16),
        scratch_shapes=[pltpu.VMEM((sources * rows, key_count), F32)],
        compiler_params=kernel_params(16),
        cost_estimate=QUICK,
        name="temporal",
    )(place, lengths, queries, own, before, before2, after)


def returned_rows(returned, x_half):
    return jnp.concatenate([returned[source, x_half] for source in range(PLANE)], axis=1)


def project_first(place, near, far, returned, wo, wo_mate):
    rows, width = near.shape[1:]
    features, cols = wo.shape
    half = features // 2
    parts = features // width - 1

    def body(place, near, far, returned, wo, wo_mate, out, weights, arrivals):
        x_place = place[1]
        sides = (wo, wo_mate)

        def fetch(part, side):
            if part == 0:
                start = pl.multiple_of(x_place * width, width)
            elif part == 1:
                start = pl.multiple_of((1 - x_place) * width, width)
            else:
                start = half + (part - 2) * width
            return pltpu.make_async_copy(
                sides[side].at[pl.ds(start, width)], weights.at[side, part], arrivals.at[side, part]
            )

        for part in range(parts):
            for side in range(2):
                fetch(part, side).start()
        lhs = [
            jnp.concatenate([near[0], near[1]], axis=0),
            jnp.concatenate([far[1], far[0]], axis=0),
            jnp.concatenate([returned_rows(returned, x_place), returned_rows(returned, 1 - x_place)], axis=0),
        ]
        for part in range(parts):
            for side in range(2):
                fetch(part, side).wait()
                product = jnp.dot(lhs[part], weights[side, part], preferred_element_type=F32)
                for which in range(2):
                    mine = product[which * rows : (which + 1) * rows]
                    out[which, side] = mine if part == 0 else out[which, side] + mine

    return pl.pallas_call(
        body,
        in_specs=[SMEM] + [WHOLE] * 3 + [IN_HBM] * 2,
        out_specs=WHOLE,
        out_shape=jax.ShapeDtypeStruct((2, 2, rows, cols), F32),
        scratch_shapes=[pltpu.VMEM((2, parts, width, cols), BF16), pltpu.SemaphoreType.DMA((2, parts))],
        compiler_params=kernel_params(WIDE),
        cost_estimate=QUICK,
        name="project_first",
    )(place, near, far, returned, wo, wo_mate)


def fetch_last(wo, wo_mate, weights, arrivals, pieces=4):
    _, width, cols = weights.shape
    first = wo.shape[0] - width
    step = width // pieces
    copies = []
    for side, source in enumerate((wo, wo_mate)):
        for piece in range(pieces):
            part = pl.ds(piece * step, step)
            copies.append(
                pltpu.make_async_copy(
                    source.at[pl.ds(first + piece * step, step)], weights.at[side, part], arrivals.at[side, piece]
                )
            )
    return copies


def finish(left, partial, weights, copies, pieces=4):
    width = weights.shape[1]
    step = width // pieces
    for side in range(2):
        total = partial[side]
        for piece in range(pieces):
            copies[side * pieces + piece].wait()
            part = slice(piece * step, (piece + 1) * step)
            total = total + jnp.dot(left[:, part], weights[side, part], preferred_element_type=F32)
        yield side, total


def project_next(place, partial, returned, wo, wo_mate):
    _, _, rows, cols = partial.shape
    width = PLANE * HS

    def body(place, partial, returned, wo, wo_mate, out, weights, arrivals):
        copies = fetch_last(wo, wo_mate, weights, arrivals)
        for copy in copies:
            copy.start()
        left = returned_rows(returned, 1 - place[1])
        for side, total in finish(left, partial[1], weights, copies):
            out[:, side * cols : (side + 1) * cols] = total.astype(BF16)

    return pl.pallas_call(
        body,
        in_specs=[SMEM] + [WHOLE] * 2 + [IN_HBM] * 2,
        out_specs=WHOLE,
        out_shape=jax.ShapeDtypeStruct((rows, 2 * cols), BF16),
        scratch_shapes=[pltpu.VMEM((2, width, cols), BF16), pltpu.SemaphoreType.DMA((2, 4))],
        compiler_params=kernel_params(WIDE),
        cost_estimate=QUICK,
        name="project_next",
    )(place, partial, returned, wo, wo_mate)


def project_own(place, partial, returned, wo, wo_mate):
    _, _, rows, cols = partial.shape
    width = PLANE * HS

    def body(place, partial, returned, wo, wo_mate, out, weights, arrivals):
        copies = fetch_last(wo, wo_mate, weights, arrivals)
        for copy in copies:
            copy.start()
        left = returned_rows(returned, place[1])
        for side, total in finish(left, partial[0], weights, copies):
            block = place[1] * C + place[2] + side * (1 - 2 * place[2])
            out[:, pl.ds(pl.multiple_of(block * cols, cols), cols)] = total.astype(BF16)

    return pl.pallas_call(
        body,
        in_specs=[SMEM] + [WHOLE] * 2 + [IN_HBM] * 2,
        out_specs=WHOLE,
        out_shape=jax.ShapeDtypeStruct((rows, XH * C * cols), BF16),
        scratch_shapes=[pltpu.VMEM((2, width, cols), BF16), pltpu.SemaphoreType.DMA((2, 4))],
        compiler_params=kernel_params(WIDE),
        cost_estimate=QUICK,
        name="project_own",
    )(place, partial, returned, wo, wo_mate)


def put_arrived(place, mixed, arrived):
    rows, width = arrived.shape
    cols = width // 2

    def body(place, mixed, arrived, out):
        out[...] = arrived[...]

    def target(side, place):
        return 0, (1 - place[1]) * C + place[2] + side * (1 - 2 * place[2])

    return pl.pallas_call(
        body,
        grid_spec=pltpu.PrefetchScalarGridSpec(
            num_scalar_prefetch=1,
            grid=(2,),
            in_specs=[ANYWHERE, pl.BlockSpec((rows, cols), lambda side, place: (0, side))],
            out_specs=pl.BlockSpec((rows, cols), target),
        ),
        out_shape=jax.ShapeDtypeStruct(mixed.shape, mixed.dtype),
        input_output_aliases={1: 0},
        compiler_params=kernel_params(16),
        cost_estimate=QUICK,
        name="put_arrived",
    )(place, mixed, arrived)


def on_device(qkv, clip_lengths, wo):
    _, frames, tok, model_width = qkv.shape
    half = model_width // 2
    quarter = half // 2
    x_place = lax.axis_index("xh")
    place = jnp.stack([lax.axis_index("z"), x_place, lax.axis_index("c")]).astype(jnp.int32)

    groups = tok // GROUP
    rows = frames * GROUP

    def by_plane(block):
        count = block.shape[0]
        heads = block.shape[3] // HS // PLANE
        split = block.reshape(count, frames, groups, GROUP, heads, PLANE, HS)
        return split.transpose(5, 0, 4, 2, 1, 3, 6).reshape(PLANE, count * heads, groups, rows, HS)

    keyvals, before = [], []
    for turn in range(ROUNDS):
        first = half + turn * PLANE * HS
        got = lax.all_to_all(by_plane(qkv[1:, :, :, first : first + PLANE * HS]), ("y", "xl"), 0, 0, tiled=True)
        keyvals.append(got)
        before.append(lax.ppermute(got, "z", [(i, (i + 1) % Z) for i in range(Z)]))
    last_two = jnp.stack([got[PLANE - 2 :] for got in keyvals])
    before2 = lax.ppermute(last_two, "z", [(i, (i + 2) % Z) for i in range(Z)])
    queries = lax.all_to_all(by_plane(qkv[:1, :, :, half:]), ("y", "xl"), 0, 0, tiled=True)

    own_cols = x_place * quarter
    far_cols = (1 - x_place) * quarter
    wo_mate = lax.ppermute(wo, "c", SWAP)
    own = lax.dynamic_slice(qkv, (0, 0, 0, own_cols), (3, frames, tok, quarter))
    far = lax.ppermute(lax.dynamic_slice(qkv, (0, 0, 0, far_cols), (3, frames, tok, quarter)), "xh", SWAP)
    mate_own = lax.ppermute(own, "c", SWAP)
    mate_far = lax.ppermute(far, "c", SWAP)
    near = spatial_attend(own, far, mate_own, mate_far, wo_mate)
    near = near.reshape(2, frames * tok, quarter)
    far = lax.ppermute(near, "xh", SWAP)

    returned = []
    after = (near, far)
    for turn in range(ROUNDS):
        mine = temporal_attend(turn, place, clip_lengths, queries, keyvals[turn], before[turn], before2, after[turn])
        sent = mine.reshape((PLANE * XH,) + mine.shape[2:])
        returned.append(lax.all_to_all(sent, ("y", "xl", "xh"), 0, 0, tiled=True).reshape(mine.shape))

    partial = project_first(place, near, far, returned[0], wo, wo_mate)
    for_next = project_next(place, partial, returned[1], wo, wo_mate)
    arrived = lax.ppermute(for_next, "xh", SWAP)
    mixed = project_own(place, partial, returned[1], wo, wo_mate)
    return put_arrived(place, mixed, arrived).reshape(frames, tok, model_width)


def solution(mesh):
    fine = Mesh(mesh.devices.reshape(Z, Y, XL, XH, C), ("z", "y", "xl", "xh", "c"))
    return jax.shard_map(
        on_device,
        mesh=fine,
        in_specs=(P(None, ("z", "y", "xl"), ("xh", "c"), None), P(), P(None, ("xh", "c"))),
        out_specs=P(("z", "y", "xl"), ("xh", "c"), None),
        check_vma=False,
    )
```

```python
import jax
import jax.numpy as jnp
import numpy as np
from jax import lax
from jax.experimental import pallas as pl
from jax.experimental.pallas import tpu as pltpu
from jax.sharding import Mesh, PartitionSpec as P

HS = 128
Z, Y, XL, XH, C = 8, 4, 2, 2, 2
PLANE = Y * XL
EXP2_SCALE = HS ** (-0.5) * float(np.log2(np.e))
F32 = jnp.float32
BF16 = jnp.bfloat16
GROUP = 8
ROUNDS = 2

SWAP = [(0, 1), (1, 0)]

SMEM = pl.BlockSpec(memory_space=pltpu.SMEM)
WHOLE = pl.BlockSpec(memory_space=pltpu.VMEM)
ANYWHERE = pl.BlockSpec(memory_space=pl.ANY)
IN_HBM = pl.BlockSpec(memory_space=pltpu.HBM)
LAST_VMEM = 44
QUICK = pl.CostEstimate(flops=1024, bytes_accessed=1024, transcendentals=0)


def kernel_params(mebibytes):
    return pltpu.CompilerParams(vmem_limit_bytes=mebibytes * 1024 * 1024)


def behind(array, *after):
    def body(*refs):
        pass

    return pl.pallas_call(
        body,
        in_specs=[ANYWHERE] * (1 + len(after)),
        out_specs=ANYWHERE,
        out_shape=jax.ShapeDtypeStruct(array.shape, array.dtype),
        input_output_aliases={0: 0},
        compiler_params=kernel_params(1),
        cost_estimate=QUICK,
        name="behind",
    )(array, *after)


def softmax_parts(scores):
    top = jnp.max(scores, axis=-1, keepdims=True)
    return jnp.exp2((scores - top) * EXP2_SCALE).astype(BF16)


def weighted(raised, values):
    both = jnp.concatenate([values, jnp.ones_like(values)], axis=1)
    result = jnp.dot(raised, both, preferred_element_type=F32)
    return result[:, :HS] / result[:, HS:]


def spatial_attend(own, far, mate_own, mate_far, after):
    _, frames, tok, width = own.shape

    def body(own, far, mate_own, mate_far, after, out):
        blocks = [(f, slice(head * HS, (head + 1) * HS)) for f in range(frames) for head in range(width // HS)]

        def keyvals_of(which, f, cols):
            return jnp.concatenate([ref[which, f, :, cols] for ref in (own, far, mate_own, mate_far)], axis=0)

        for first in range(0, len(blocks), 8):
            batch = blocks[first : first + 8]
            scores = []
            for f, cols in batch:
                queries = jnp.concatenate([own[0, f, :, cols], far[0, f, :, cols]], axis=0)
                scores.append(
                    lax.dot_general(
                        queries, keyvals_of(1, f, cols), (((1,), (1,)), ((), ())), preferred_element_type=F32
                    )
                )
            raised = [softmax_parts(block) for block in scores]
            results = [weighted(block, keyvals_of(2, f, cols)).astype(BF16) for block, (f, cols) in zip(raised, batch)]
            for result, (f, cols) in zip(results, batch):
                out[0, f, :, cols] = result[:tok]
                out[1, f, :, cols] = result[tok:]

    return pl.pallas_call(
        body,
        in_specs=[WHOLE] * 4 + [ANYWHERE],
        out_specs=WHOLE,
        out_shape=jax.ShapeDtypeStruct((2, frames, tok, width), BF16),
        compiler_params=kernel_params(16),
        cost_estimate=QUICK,
        name="spatial",
    )(own, far, mate_own, mate_far, after)


def temporal_scores(clips, place, lengths, queries, keyvals, first_query, first_key, bias, store):
    _, _, groups, rows, _ = queries.shape
    frames_dev = rows // GROUP
    query_rows, key_count = bias.shape
    first = place[0] * (PLANE * frames_dev)

    row = lax.broadcasted_iota(jnp.int32, (query_rows, 1), 0)
    frame = first + first_query * frames_dev + row // GROUP
    start = jnp.zeros_like(frame)
    begin = jnp.int32(0)
    for clip in range(clips):
        start = jnp.where(frame >= begin, begin, start)
        begin = begin + lengths[clip]
    oldest = first + first_key * frames_dev
    token = (row % GROUP) * 4096
    low = token + start - oldest
    high = token + frame - oldest
    col = lax.broadcasted_iota(jnp.int32, (1, key_count), 1)
    code = (col % GROUP) * 4096 + col // GROUP
    bias[...] = jnp.where((code >= low) & (code <= high), 0.0, -1e30)

    blocks = slice(first_query, first_query + query_rows // rows)
    for turn in range(ROUNDS):
        pieces = []
        for group in range(groups):
            def rows_of(which):
                return jnp.concatenate([part[:, which, group].reshape(-1, HS) for part in keyvals[turn]], axis=0)

            asked = queries[blocks, turn, group].reshape(-1, HS)
            scores = lax.dot_general(asked, rows_of(0), (((1,), (1,)), ((), ())), preferred_element_type=F32)
            result = weighted(softmax_parts(scores + bias[...]), rows_of(1))
            pieces.append(result.reshape(-1, 1, GROUP, HS))
        joined = jnp.concatenate(pieces, axis=1).reshape(-1, frames_dev * groups * GROUP, HS).astype(BF16)
        store(turn, joined)


EARLY = 2


def temporal_late(place, lengths, queries, own, before):
    sources, _, groups, rows, _ = queries.shape
    clips = lengths.shape[0]

    def body(place, lengths, queries, *refs):
        own, before = refs[:ROUNDS], refs[ROUNDS : 2 * ROUNDS]
        out, bias = refs[2 * ROUNDS :]

        def store(turn, joined):
            for copy in range(XH):
                out[EARLY:, copy, :, turn * HS : (turn + 1) * HS] = joined

        keyvals = [(before[turn], own[turn]) for turn in range(ROUNDS)]
        temporal_scores(clips, place, lengths, queries, keyvals, EARLY, -sources, bias, store)

    return pl.pallas_call(
        body,
        in_specs=[SMEM, SMEM] + [WHOLE] * (1 + 2 * ROUNDS),
        out_specs=WHOLE,
        out_shape=jax.ShapeDtypeStruct((sources, XH, groups * rows, ROUNDS * HS), BF16),
        scratch_shapes=[pltpu.VMEM(((sources - EARLY) * rows, 2 * sources * rows), F32)],
        compiler_params=kernel_params(12),
        cost_estimate=QUICK,
        name="temporal_late",
    )(place, lengths, queries, *own, *before)


def temporal_early(place, lengths, queries, own, before, before2, late, after):
    sources, _, groups, rows, _ = queries.shape
    clips = lengths.shape[0]

    def body(place, lengths, queries, *refs):
        own, before, before2 = (refs[part * ROUNDS : (part + 1) * ROUNDS] for part in range(3))
        out, bias = refs[-2:]

        def store(turn, joined):
            for copy in range(XH):
                out[:, copy, :, turn * HS : (turn + 1) * HS] = joined

        keyvals = [(before2[turn], before[turn], own[turn].at[:EARLY]) for turn in range(ROUNDS)]
        temporal_scores(clips, place, lengths, queries, keyvals, 0, -sources - EARLY, bias, store)

    block = (EARLY,) + late.shape[1:]
    return pl.pallas_call(
        body,
        grid=(1,),
        in_specs=[SMEM, SMEM] + [WHOLE] * (1 + 3 * ROUNDS) + [ANYWHERE] * 2,
        out_specs=pl.BlockSpec(block, lambda step: (0, 0, 0, 0)),
        out_shape=jax.ShapeDtypeStruct(late.shape, BF16),
        scratch_shapes=[pltpu.VMEM((EARLY * rows, (sources + 2 * EARLY) * rows), F32)],
        input_output_aliases={3 + 3 * ROUNDS: 0},
        compiler_params=kernel_params(12),
        cost_estimate=QUICK,
        name="temporal_early",
    )(place, lengths, queries, *own, *before, *before2, late, after)


def returned_rows(returned, x_half):
    return jnp.concatenate([returned[source, x_half] for source in range(PLANE)], axis=1)


def fetch_rows(sources, starts, targets, arrivals):
    return [
        pltpu.make_async_copy(source.at[pl.ds(start, targets.shape[2])], targets.at[side, part], arrivals.at[side, part])
        for part, start in enumerate(starts)
        for side, source in enumerate(sources)
    ]


def project_first(place, near, far, wo, wo_mate):
    rows, width = near.shape[1:]
    cols = wo.shape[1]

    def body(place, near, far, wo, wo_mate, out, weights, arrivals):
        x_place = place[1]
        starts = [pl.multiple_of(x_place * width, width), pl.multiple_of((1 - x_place) * width, width)]
        copies = fetch_rows((wo, wo_mate), starts, weights, arrivals)
        for copy in copies:
            copy.start()
        lhs = [
            jnp.concatenate([near[0], near[1]], axis=0),
            jnp.concatenate([far[1], far[0]], axis=0),
        ]
        for part in range(2):
            for side in range(2):
                copies[part * 2 + side].wait()
                product = jnp.dot(lhs[part], weights[side, part], preferred_element_type=F32)
                for which in range(2):
                    mine = product[which * rows : (which + 1) * rows]
                    out[which, side] = mine if part == 0 else out[which, side] + mine

    return pl.pallas_call(
        body,
        in_specs=[SMEM] + [WHOLE] * 2 + [IN_HBM] * 2,
        out_specs=WHOLE,
        out_shape=jax.ShapeDtypeStruct((2, 2, rows, cols), F32),
        scratch_shapes=[pltpu.VMEM((2, 2, width, cols), BF16), pltpu.SemaphoreType.DMA((2, 2))],
        compiler_params=kernel_params(LAST_VMEM),
        cost_estimate=QUICK,
        name="project_first",
    )(place, near, far, wo, wo_mate)


def project_last(name, which, place, partial, returned, wo, wo_mate, out_cols, store):
    _, _, rows, cols = partial.shape
    half = wo.shape[0] // 2
    parts = 4
    step = half // parts

    def body(place, partial, returned, wo, wo_mate, out, weights, arrivals):
        copies = fetch_rows((wo, wo_mate), [half + part * step for part in range(parts)], weights, arrivals)
        for copy in copies:
            copy.start()
        left = returned_rows(returned, 1 - place[1] if which else place[1])
        total = [partial[which, 0], partial[which, 1]]
        for part in range(parts):
            for side in range(2):
                copies[part * 2 + side].wait()
                block = left[:, part * step : (part + 1) * step]
                total[side] = total[side] + jnp.dot(block, weights[side, part], preferred_element_type=F32)
        for side in range(2):
            store(place, out, side, total[side].astype(BF16))

    return pl.pallas_call(
        body,
        in_specs=[SMEM] + [WHOLE] * 2 + [IN_HBM] * 2,
        out_specs=WHOLE,
        out_shape=jax.ShapeDtypeStruct((rows, out_cols), BF16),
        scratch_shapes=[pltpu.VMEM((2, parts, step, cols), BF16), pltpu.SemaphoreType.DMA((2, parts))],
        compiler_params=kernel_params(LAST_VMEM),
        cost_estimate=QUICK,
        name=name,
    )(place, partial, returned, wo, wo_mate)


def project_next(place, partial, returned, wo, wo_mate):
    cols = wo.shape[1]

    def store(place, out, side, block):
        out[:, side * cols : (side + 1) * cols] = block

    return project_last("project_next", 1, place, partial, returned, wo, wo_mate, 2 * cols, store)


def project_own(place, partial, returned, wo, wo_mate):
    cols = wo.shape[1]

    def store(place, out, side, block):
        target = place[1] * C + place[2] + side * (1 - 2 * place[2])
        out[:, pl.ds(pl.multiple_of(target * cols, cols), cols)] = block

    return project_last("project_own", 0, place, partial, returned, wo, wo_mate, XH * C * cols, store)


def put_arrived(place, mixed, arrived):
    rows, width = arrived.shape
    cols = width // 2

    def body(place, mixed, arrived, out):
        out[...] = arrived[...]

    def target(side, place):
        return 0, (1 - place[1]) * C + place[2] + side * (1 - 2 * place[2])

    return pl.pallas_call(
        body,
        grid_spec=pltpu.PrefetchScalarGridSpec(
            num_scalar_prefetch=1,
            grid=(2,),
            in_specs=[ANYWHERE, pl.BlockSpec((rows, cols), lambda side, place: (0, side))],
            out_specs=pl.BlockSpec((rows, cols), target),
        ),
        out_shape=jax.ShapeDtypeStruct(mixed.shape, mixed.dtype),
        input_output_aliases={1: 0},
        compiler_params=kernel_params(16),
        cost_estimate=QUICK,
        name="put_arrived",
    )(place, mixed, arrived)


def on_device(qkv, clip_lengths, wo):
    _, frames, tok, model_width = qkv.shape
    half = model_width // 2
    quarter = half // 2
    x_place = lax.axis_index("xh")
    place = jnp.stack([lax.axis_index("z"), x_place, lax.axis_index("c")]).astype(jnp.int32)

    groups = tok // GROUP
    rows = frames * GROUP

    def by_plane(block, turn=None):
        split = block.reshape(block.shape[0], frames, groups, GROUP, PLANE, ROUNDS, HS)
        if turn is not None:
            split = split[:, :, :, :, :, turn : turn + 1]
        return split.transpose(4, 0, 5, 2, 1, 3, 6).reshape(PLANE, -1, groups, rows, HS)

    onward = [(i, (i + 1) % Z) for i in range(Z)]
    keyvals, before, before2 = [], [], []
    for turn in range(ROUNDS):
        got = lax.all_to_all(by_plane(qkv[1:, :, :, half:], turn), ("y", "xl"), 0, 0, tiled=True)
        keyvals.append(got)
        before.append(lax.ppermute(got, "z", onward))
        before2.append(lax.ppermute(before[-1][PLANE - EARLY :], "z", onward))
    own_cols = x_place * quarter
    far_cols = (1 - x_place) * quarter
    wo_mate = lax.ppermute(wo, "c", SWAP)
    own = lax.dynamic_slice(qkv, (0, 0, 0, own_cols), (3, frames, tok, quarter))
    far = lax.ppermute(lax.dynamic_slice(qkv, (0, 0, 0, far_cols), (3, frames, tok, quarter)), "xh", SWAP)
    mate_own = lax.ppermute(own, "c", SWAP)
    mate_far = lax.ppermute(far, "c", SWAP)
    near = spatial_attend(own, far, mate_own, mate_far, wo_mate)
    near = near.reshape(2, frames * tok, quarter)
    far = lax.ppermute(near, "xh", SWAP)

    queries = by_plane(qkv[:1, :, :, half:])
    queries = lax.all_to_all(queries, ("y", "xl"), 0, 0, tiled=True)
    mine = temporal_late(place, clip_lengths, queries, keyvals, before)
    mine = temporal_early(place, clip_lengths, queries, keyvals, before, before2, mine, far)
    sent = mine.reshape((PLANE * XH,) + mine.shape[2:])
    returned = lax.all_to_all(sent, ("y", "xl", "xh"), 0, 0, tiled=True).reshape(mine.shape)

    partial = project_first(place, near, far, wo, wo_mate)
    for_next = project_next(place, partial, returned, wo, wo_mate)
    arrived = lax.ppermute(for_next, "xh", SWAP)
    mixed = project_own(place, partial, returned, wo, wo_mate)
    return put_arrived(place, mixed, arrived).reshape(frames, tok, model_width)


def solution(mesh):
    fine = Mesh(mesh.devices.reshape(Z, Y, XL, XH, C), ("z", "y", "xl", "xh", "c"))
    return jax.shard_map(
        on_device,
        mesh=fine,
        in_specs=(P(None, ("z", "y", "xl"), ("xh", "c"), None), P(), P(None, ("xh", "c"))),
        out_specs=P(("z", "y", "xl"), ("xh", "c"), None),
        check_vma=False,
    )
```

```python
import jax
import jax.numpy as jnp
import numpy as np
from jax import lax
from jax.experimental import pallas as pl
from jax.experimental.pallas import tpu as pltpu
from jax.sharding import Mesh, PartitionSpec as P

HS = 128
Z, Y, XL, XH, C = 8, 4, 2, 2, 2
PLANE = Y * XL
EXP2_SCALE = HS ** (-0.5) * float(np.log2(np.e))
F32 = jnp.float32
BF16 = jnp.bfloat16
GROUP = 8
ROUNDS = 2

SWAP = [(0, 1), (1, 0)]

SMEM = pl.BlockSpec(memory_space=pltpu.SMEM)
WHOLE = pl.BlockSpec(memory_space=pltpu.VMEM)
ANYWHERE = pl.BlockSpec(memory_space=pl.ANY)
IN_HBM = pl.BlockSpec(memory_space=pltpu.HBM)
PACK_VMEM = 60
LAST_VMEM = 44
QUICK = pl.CostEstimate(flops=1024, bytes_accessed=1024, transcendentals=0)


def kernel_params(mebibytes):
    return pltpu.CompilerParams(vmem_limit_bytes=mebibytes * 1024 * 1024)


def behind(array, *after):
    def body(*refs):
        pass

    return pl.pallas_call(
        body,
        in_specs=[ANYWHERE] * (1 + len(after)),
        out_specs=ANYWHERE,
        out_shape=jax.ShapeDtypeStruct(array.shape, array.dtype),
        input_output_aliases={0: 0},
        compiler_params=kernel_params(1),
        cost_estimate=QUICK,
        name="behind",
    )(array, *after)


def softmax_parts(scores):
    top = jnp.max(scores, axis=-1, keepdims=True)
    return jnp.exp2((scores - top) * EXP2_SCALE).astype(BF16)


def weighted(raised, values):
    both = jnp.concatenate([values, jnp.ones_like(values)], axis=1)
    result = jnp.dot(raised, both, preferred_element_type=F32)
    return result[:, :HS] / result[:, HS:]


def pack_rest(qkv):
    _, frames, tok, model_width = qkv.shape
    half = model_width // 2
    groups = tok // GROUP
    step = 2

    def body(qkv, queries, keyvals):
        for device in range(PLANE):
            for slot in range(ROUNDS + 2):
                which, turn = (0, slot) if slot < ROUNDS else (slot - ROUNDS + 1, ROUNDS - 1)
                target, place = (queries, slot) if slot < ROUNDS else (keyvals, slot - ROUNDS)
                first = (device * ROUNDS + turn) * HS
                block = qkv[which, :, :, first : first + HS].astype(F32).reshape(step, groups, GROUP, HS)
                for group in range(groups):
                    target[device, place, group] = block[:, group].reshape(step * GROUP, HS).astype(BF16)

    rows = jax.ShapeDtypeStruct((PLANE, 2, groups, frames * GROUP, HS), BF16)
    rows_spec = pl.BlockSpec((PLANE, 2, groups, step * GROUP, HS), lambda f: (0, 0, 0, f, 0))
    return pl.pallas_call(
        body,
        grid=(frames // step,),
        in_specs=[pl.BlockSpec((3, step, tok, half), lambda f: (0, f, 0, 1))],
        out_specs=[rows_spec] * 2,
        out_shape=[rows] * 2,
        compiler_params=kernel_params(PACK_VMEM),
        cost_estimate=QUICK,
        name="pack_rest",
    )(qkv)


def spatial_attend(own, far, mate_own, mate_far, after):
    _, frames, tok, width = own.shape

    def body(own, far, mate_own, mate_far, after, out):
        blocks = [(f, slice(head * HS, (head + 1) * HS)) for f in range(frames) for head in range(width // HS)]

        def keyvals_of(which, f, cols):
            return jnp.concatenate([ref[which, f, :, cols] for ref in (own, far, mate_own, mate_far)], axis=0)

        for first in range(0, len(blocks), 8):
            batch = blocks[first : first + 8]
            scores = []
            for f, cols in batch:
                queries = jnp.concatenate([own[0, f, :, cols], far[0, f, :, cols]], axis=0)
                scores.append(
                    lax.dot_general(
                        queries, keyvals_of(1, f, cols), (((1,), (1,)), ((), ())), preferred_element_type=F32
                    )
                )
            raised = [softmax_parts(block) for block in scores]
            results = [weighted(block, keyvals_of(2, f, cols)).astype(BF16) for block, (f, cols) in zip(raised, batch)]
            for result, (f, cols) in zip(results, batch):
                out[0, f, :, cols] = result[:tok]
                out[1, f, :, cols] = result[tok:]

    return pl.pallas_call(
        body,
        in_specs=[WHOLE] * 4 + [ANYWHERE],
        out_specs=WHOLE,
        out_shape=jax.ShapeDtypeStruct((2, frames, tok, width), BF16),
        compiler_params=kernel_params(16),
        cost_estimate=QUICK,
        name="spatial",
    )(own, far, mate_own, mate_far, after)


def temporal_scores(clips, place, lengths, queries, keyvals, first_query, first_key, bias, batch, store):
    _, _, groups, rows, _ = queries.shape
    frames_dev = rows // GROUP
    query_rows, key_count = bias.shape
    first = place[0] * (PLANE * frames_dev)

    row = lax.broadcasted_iota(jnp.int32, (query_rows, 1), 0)
    frame = first + first_query * frames_dev + row // GROUP
    start = jnp.zeros_like(frame)
    begin = jnp.int32(0)
    for clip in range(clips):
        start = jnp.where(frame >= begin, begin, start)
        begin = begin + lengths[clip]
    oldest = first + first_key * frames_dev
    token = (row % GROUP) * 4096
    low = token + start - oldest
    high = token + frame - oldest
    col = lax.broadcasted_iota(jnp.int32, (1, key_count), 1)
    code = (col % GROUP) * 4096 + col // GROUP
    bias[...] = jnp.where((code >= low) & (code <= high), 0.0, -1e30)

    blocks = slice(first_query, first_query + query_rows // rows)
    def rows_of(which, turn, group):
        return jnp.concatenate([part[:, which, group].reshape(-1, HS) for part in keyvals[turn]], axis=0)

    units = [(turn, group) for turn in range(ROUNDS) for group in range(groups)]
    for first_unit in range(0, len(units), batch):
        some = units[first_unit : first_unit + batch]
        scores = [
            lax.dot_general(
                queries[blocks, turn, group].reshape(-1, HS),
                rows_of(0, turn, group),
                (((1,), (1,)), ((), ())),
                preferred_element_type=F32,
            )
            for turn, group in some
        ]
        raised = [softmax_parts(block + bias[...]) for block in scores]
        results = [weighted(block, rows_of(1, turn, group)) for block, (turn, group) in zip(raised, some)]
        for at in range(0, len(some), groups):
            pieces = [result.reshape(-1, 1, GROUP, HS) for result in results[at : at + groups]]
            joined = jnp.concatenate(pieces, axis=1).reshape(-1, frames_dev * groups * GROUP, HS).astype(BF16)
            store(some[at][0], joined)


EARLY = 2


def temporal_late(place, lengths, queries, own, before):
    sources, _, groups, rows, _ = queries.shape
    clips = lengths.shape[0]

    def body(place, lengths, queries, *refs):
        own, before = refs[:ROUNDS], refs[ROUNDS : 2 * ROUNDS]
        out, bias = refs[2 * ROUNDS :]

        def store(turn, joined):
            for copy in range(XH):
                out[EARLY:, copy, :, turn * HS : (turn + 1) * HS] = joined

        keyvals = [(before[turn], own[turn]) for turn in range(ROUNDS)]
        temporal_scores(clips, place, lengths, queries, keyvals, EARLY, -sources, bias, groups, store)

    return pl.pallas_call(
        body,
        in_specs=[SMEM, SMEM] + [WHOLE] * (1 + 2 * ROUNDS),
        out_specs=WHOLE,
        out_shape=jax.ShapeDtypeStruct((sources, XH, groups * rows, ROUNDS * HS), BF16),
        scratch_shapes=[pltpu.VMEM(((sources - EARLY) * rows, 2 * sources * rows), F32)],
        compiler_params=kernel_params(12),
        cost_estimate=QUICK,
        name="temporal_late",
    )(place, lengths, queries, *own, *before)


def temporal_early(place, lengths, queries, own, before, before2, late, after):
    sources, _, groups, rows, _ = queries.shape
    clips = lengths.shape[0]

    def body(place, lengths, queries, *refs):
        own, before, before2 = (refs[part * ROUNDS : (part + 1) * ROUNDS] for part in range(3))
        out, bias = refs[-2:]

        def store(turn, joined):
            for copy in range(XH):
                out[:, copy, :, turn * HS : (turn + 1) * HS] = joined

        keyvals = [(before2[turn], before[turn], own[turn].at[:EARLY]) for turn in range(ROUNDS)]
        temporal_scores(clips, place, lengths, queries, keyvals, 0, -sources - EARLY, bias, ROUNDS * groups, store)

    block = (EARLY,) + late.shape[1:]
    return pl.pallas_call(
        body,
        grid=(1,),
        in_specs=[SMEM, SMEM] + [WHOLE] * (1 + 3 * ROUNDS) + [ANYWHERE] * 2,
        out_specs=pl.BlockSpec(block, lambda step: (0, 0, 0, 0)),
        out_shape=jax.ShapeDtypeStruct(late.shape, BF16),
        scratch_shapes=[pltpu.VMEM((EARLY * rows, (sources + 2 * EARLY) * rows), F32)],
        input_output_aliases={3 + 3 * ROUNDS: 0},
        compiler_params=kernel_params(12),
        cost_estimate=QUICK,
        name="temporal_early",
    )(place, lengths, queries, *own, *before, *before2, late, after)


def returned_rows(returned, x_half):
    return jnp.concatenate([returned[source, x_half] for source in range(PLANE)], axis=1)


def fetch_rows(sources, starts, targets, arrivals):
    return [
        pltpu.make_async_copy(source.at[pl.ds(start, targets.shape[2])], targets.at[side, part], arrivals.at[side, part])
        for part, start in enumerate(starts)
        for side, source in enumerate(sources)
    ]


def project_first(place, near, far, wo, wo_mate):
    rows, width = near.shape[1:]
    cols = wo.shape[1]

    def body(place, near, far, wo, wo_mate, out, weights, arrivals):
        x_place = place[1]
        starts = [pl.multiple_of(x_place * width, width), pl.multiple_of((1 - x_place) * width, width)]
        copies = fetch_rows((wo, wo_mate), starts, weights, arrivals)
        for copy in copies:
            copy.start()
        lhs = [
            jnp.concatenate([near[0], near[1]], axis=0),
            jnp.concatenate([far[1], far[0]], axis=0),
        ]
        for part in range(2):
            for side in range(2):
                copies[part * 2 + side].wait()
                product = jnp.dot(lhs[part], weights[side, part], preferred_element_type=F32)
                for which in range(2):
                    mine = product[which * rows : (which + 1) * rows]
                    out[which, side] = mine if part == 0 else out[which, side] + mine

    return pl.pallas_call(
        body,
        in_specs=[SMEM] + [WHOLE] * 2 + [IN_HBM] * 2,
        out_specs=WHOLE,
        out_shape=jax.ShapeDtypeStruct((2, 2, rows, cols), F32),
        scratch_shapes=[pltpu.VMEM((2, 2, width, cols), BF16), pltpu.SemaphoreType.DMA((2, 2))],
        compiler_params=kernel_params(LAST_VMEM),
        cost_estimate=QUICK,
        name="project_first",
    )(place, near, far, wo, wo_mate)


def project_last(name, which, place, partial, returned, wo, wo_mate, out_cols, store):
    _, _, rows, cols = partial.shape
    half = wo.shape[0] // 2
    parts = 4
    step = half // parts

    def body(place, partial, returned, wo, wo_mate, out, weights, arrivals):
        copies = fetch_rows((wo, wo_mate), [half + part * step for part in range(parts)], weights, arrivals)
        for copy in copies:
            copy.start()
        left = returned_rows(returned, 1 - place[1] if which else place[1])
        total = [partial[which, 0], partial[which, 1]]
        for part in range(parts):
            for side in range(2):
                copies[part * 2 + side].wait()
                block = left[:, part * step : (part + 1) * step]
                total[side] = total[side] + jnp.dot(block, weights[side, part], preferred_element_type=F32)
        for side in range(2):
            store(place, out, side, total[side].astype(BF16))

    return pl.pallas_call(
        body,
        in_specs=[SMEM] + [WHOLE] * 2 + [IN_HBM] * 2,
        out_specs=WHOLE,
        out_shape=jax.ShapeDtypeStruct((rows, out_cols), BF16),
        scratch_shapes=[pltpu.VMEM((2, parts, step, cols), BF16), pltpu.SemaphoreType.DMA((2, parts))],
        compiler_params=kernel_params(LAST_VMEM),
        cost_estimate=QUICK,
        name=name,
    )(place, partial, returned, wo, wo_mate)


def project_next(place, partial, returned, wo, wo_mate):
    cols = wo.shape[1]

    def store(place, out, side, block):
        out[:, side * cols : (side + 1) * cols] = block

    return project_last("project_next", 1, place, partial, returned, wo, wo_mate, 2 * cols, store)


def project_own(place, partial, returned, wo, wo_mate):
    cols = wo.shape[1]

    def store(place, out, side, block):
        target = place[1] * C + place[2] + side * (1 - 2 * place[2])
        out[:, pl.ds(pl.multiple_of(target * cols, cols), cols)] = block

    return project_last("project_own", 0, place, partial, returned, wo, wo_mate, XH * C * cols, store)


def put_arrived(place, mixed, arrived):
    rows, width = arrived.shape
    cols = width // 2

    def body(place, mixed, arrived, out):
        out[...] = arrived[...]

    def target(side, place):
        return 0, (1 - place[1]) * C + place[2] + side * (1 - 2 * place[2])

    return pl.pallas_call(
        body,
        grid_spec=pltpu.PrefetchScalarGridSpec(
            num_scalar_prefetch=1,
            grid=(2,),
            in_specs=[ANYWHERE, pl.BlockSpec((rows, cols), lambda side, place: (0, side))],
            out_specs=pl.BlockSpec((rows, cols), target),
        ),
        out_shape=jax.ShapeDtypeStruct(mixed.shape, mixed.dtype),
        input_output_aliases={1: 0},
        compiler_params=kernel_params(16),
        cost_estimate=QUICK,
        name="put_arrived",
    )(place, mixed, arrived)


def on_device(qkv, clip_lengths, wo):
    _, frames, tok, model_width = qkv.shape
    half = model_width // 2
    quarter = half // 2
    x_place = lax.axis_index("xh")
    place = jnp.stack([lax.axis_index("z"), x_place, lax.axis_index("c")]).astype(jnp.int32)

    groups = tok // GROUP
    rows = frames * GROUP

    def by_plane(block, turn):
        split = block.reshape(block.shape[0], frames, groups, GROUP, PLANE, ROUNDS, HS)[:, :, :, :, :, turn]
        return split.transpose(4, 0, 2, 1, 3, 5).reshape(PLANE, -1, groups, rows, HS)

    onward = [(i, (i + 1) % Z) for i in range(Z)]
    queries, last_packed = pack_rest(qkv)
    packed = (by_plane(qkv[1:, :, :, half:], 0), last_packed)
    arrived = [lax.all_to_all(block, ("y", "xl"), 0, 0, tiled=True) for block in packed]

    own_cols = x_place * quarter
    far_cols = (1 - x_place) * quarter
    wo_mate = lax.ppermute(wo, "c", SWAP)
    own = lax.dynamic_slice(qkv, (0, 0, 0, own_cols), (3, frames, tok, quarter))
    far = lax.ppermute(lax.dynamic_slice(qkv, (0, 0, 0, far_cols), (3, frames, tok, quarter)), "xh", SWAP)
    mate_own = lax.ppermute(own, "c", SWAP)
    mate_far = lax.ppermute(far, "c", SWAP)
    near = spatial_attend(own, far, mate_own, mate_far, wo_mate)
    near = near.reshape(2, frames * tok, quarter)
    far = lax.ppermute(near, "xh", SWAP)

    keyvals, before, before2 = [], [], []
    for turn, got in enumerate(arrived):
        if turn:
            got = behind(got, near)
        keyvals.append(got)
        before.append(lax.ppermute(got, "z", onward))
        before2.append(lax.ppermute(before[-1][PLANE - EARLY :], "z", onward))

    queries = lax.all_to_all(queries, ("y", "xl"), 0, 0, tiled=True)
    mine = temporal_late(place, clip_lengths, queries, keyvals, before)
    mine = temporal_early(place, clip_lengths, queries, keyvals, before, before2, mine, far)
    sent = mine.reshape((PLANE * XH,) + mine.shape[2:])
    returned = lax.all_to_all(sent, ("y", "xl", "xh"), 0, 0, tiled=True).reshape(mine.shape)

    partial = project_first(place, near, far, wo, wo_mate)
    for_next = project_next(place, partial, returned, wo, wo_mate)
    arrived = lax.ppermute(for_next, "xh", SWAP)
    mixed = project_own(place, partial, returned, wo, wo_mate)
    return put_arrived(place, mixed, arrived).reshape(frames, tok, model_width)


def solution(mesh):
    fine = Mesh(mesh.devices.reshape(Z, Y, XL, XH, C), ("z", "y", "xl", "xh", "c"))
    return jax.shard_map(
        on_device,
        mesh=fine,
        in_specs=(P(None, ("z", "y", "xl"), ("xh", "c"), None), P(), P(None, ("xh", "c"))),
        out_specs=P(("z", "y", "xl"), ("xh", "c"), None),
        check_vma=False,
    )
```

```python
import jax
import jax.numpy as jnp
import numpy as np
from jax import lax
from jax.experimental import pallas as pl
from jax.experimental.pallas import tpu as pltpu
from jax.sharding import Mesh, PartitionSpec as P

HS = 128
Z, Y, XL, XH, C = 8, 4, 2, 2, 2
PLANE = Y * XL
EXP2_SCALE = HS ** (-0.5) * float(np.log2(np.e))
F32 = jnp.float32
BF16 = jnp.bfloat16
GROUP = 8
ROUNDS = 2

SWAP = [(0, 1), (1, 0)]

SMEM = pl.BlockSpec(memory_space=pltpu.SMEM)
WHOLE = pl.BlockSpec(memory_space=pltpu.VMEM)
ANYWHERE = pl.BlockSpec(memory_space=pl.ANY)
IN_HBM = pl.BlockSpec(memory_space=pltpu.HBM)
PACK_VMEM = 60
LAST_VMEM = 44
QUICK = pl.CostEstimate(flops=1024, bytes_accessed=1024, transcendentals=0)


def kernel_params(mebibytes):
    return pltpu.CompilerParams(vmem_limit_bytes=mebibytes * 1024 * 1024)


def behind(array, *after):
    def body(*refs):
        pass

    return pl.pallas_call(
        body,
        in_specs=[ANYWHERE] * (1 + len(after)),
        out_specs=ANYWHERE,
        out_shape=jax.ShapeDtypeStruct(array.shape, array.dtype),
        input_output_aliases={0: 0},
        compiler_params=kernel_params(1),
        cost_estimate=QUICK,
        name="behind",
    )(array, *after)


def softmax_parts(scores):
    top = jnp.max(scores, axis=-1, keepdims=True)
    return jnp.exp2((scores - top) * EXP2_SCALE).astype(BF16)


def weighted(raised, values):
    both = jnp.concatenate([values, jnp.ones_like(values)], axis=1)
    result = jnp.dot(raised, both, preferred_element_type=F32)
    return result[:, :HS] / result[:, HS:]


def pack_rest(qkv):
    _, frames, tok, model_width = qkv.shape
    half = model_width // 2
    groups = tok // GROUP
    step = 2

    def body(qkv, queries, keyvals):
        for device in range(PLANE):
            for slot in range(ROUNDS + 2):
                which, turn = (0, slot) if slot < ROUNDS else (slot - ROUNDS + 1, ROUNDS - 1)
                target, place = (queries, slot) if slot < ROUNDS else (keyvals, slot - ROUNDS)
                first = (device * ROUNDS + turn) * HS
                block = qkv[which, :, :, first : first + HS].astype(F32).reshape(step, groups, GROUP, HS)
                for group in range(groups):
                    target[device, place, group] = block[:, group].reshape(step * GROUP, HS).astype(BF16)

    rows = jax.ShapeDtypeStruct((PLANE, 2, groups, frames * GROUP, HS), BF16)
    rows_spec = pl.BlockSpec((PLANE, 2, groups, step * GROUP, HS), lambda f: (0, 0, 0, f, 0))
    return pl.pallas_call(
        body,
        grid=(frames // step,),
        in_specs=[pl.BlockSpec((3, step, tok, half), lambda f: (0, f, 0, 1))],
        out_specs=[rows_spec] * 2,
        out_shape=[rows] * 2,
        compiler_params=kernel_params(PACK_VMEM),
        cost_estimate=QUICK,
        name="pack_rest",
    )(qkv)


def spatial_attend(own, far, mate_own, mate_far, after):
    _, frames, tok, width = own.shape

    def body(own, far, mate_own, mate_far, after, out):
        blocks = [(f, slice(head * HS, (head + 1) * HS)) for f in range(frames) for head in range(width // HS)]

        def keyvals_of(which, f, cols):
            return jnp.concatenate([ref[which, f, :, cols] for ref in (own, far, mate_own, mate_far)], axis=0)

        for first in range(0, len(blocks), 8):
            batch = blocks[first : first + 8]
            scores = []
            for f, cols in batch:
                queries = jnp.concatenate([own[0, f, :, cols], far[0, f, :, cols]], axis=0)
                scores.append(
                    lax.dot_general(
                        queries, keyvals_of(1, f, cols), (((1,), (1,)), ((), ())), preferred_element_type=F32
                    )
                )
            raised = [softmax_parts(block) for block in scores]
            results = [weighted(block, keyvals_of(2, f, cols)).astype(BF16) for block, (f, cols) in zip(raised, batch)]
            for result, (f, cols) in zip(results, batch):
                out[0, f, :, cols] = result[:tok]
                out[1, f, :, cols] = result[tok:]

    return pl.pallas_call(
        body,
        in_specs=[WHOLE] * 4 + [ANYWHERE],
        out_specs=WHOLE,
        out_shape=jax.ShapeDtypeStruct((2, frames, tok, width), BF16),
        compiler_params=kernel_params(16),
        cost_estimate=QUICK,
        name="spatial",
    )(own, far, mate_own, mate_far, after)


def temporal_scores(clips, place, lengths, queries, keyvals, first_query, first_key, bias, batch, store):
    _, _, groups, rows, _ = queries.shape
    frames_dev = rows // GROUP
    query_rows, key_count = bias.shape
    first = place[0] * (PLANE * frames_dev)

    row = lax.broadcasted_iota(jnp.int32, (query_rows, 1), 0)
    frame = first + first_query * frames_dev + row // GROUP
    start = jnp.zeros_like(frame)
    begin = jnp.int32(0)
    for clip in range(clips):
        start = jnp.where(frame >= begin, begin, start)
        begin = begin + lengths[clip]
    oldest = first + first_key * frames_dev
    token = (row % GROUP) * 4096
    low = token + start - oldest
    high = token + frame - oldest
    col = lax.broadcasted_iota(jnp.int32, (1, key_count), 1)
    code = (col % GROUP) * 4096 + col // GROUP
    bias[...] = jnp.where((code >= low) & (code <= high), 0.0, -1e30)

    blocks = slice(first_query, first_query + query_rows // rows)
    def rows_of(which, turn, group):
        return jnp.concatenate([part[:, which, group].reshape(-1, HS) for part in keyvals[turn]], axis=0)

    units = [(turn, group) for turn in range(ROUNDS) for group in range(groups)]
    for first_unit in range(0, len(units), batch):
        some = units[first_unit : first_unit + batch]
        scores = [
            lax.dot_general(
                queries[blocks, turn, group].reshape(-1, HS),
                rows_of(0, turn, group),
                (((1,), (1,)), ((), ())),
                preferred_element_type=F32,
            )
            for turn, group in some
        ]
        raised = [softmax_parts(block + bias[...]) for block in scores]
        results = [weighted(block, rows_of(1, turn, group)) for block, (turn, group) in zip(raised, some)]
        for at in range(0, len(some), groups):
            pieces = [result.reshape(-1, 1, GROUP, HS) for result in results[at : at + groups]]
            joined = jnp.concatenate(pieces, axis=1).reshape(-1, frames_dev * groups * GROUP, HS).astype(BF16)
            store(some[at][0], joined)


EARLY = 2


def temporal_late(place, lengths, queries, own, before):
    sources, _, groups, rows, _ = queries.shape
    clips = lengths.shape[0]

    def body(place, lengths, queries, *refs):
        own, before = refs[:ROUNDS], refs[ROUNDS : 2 * ROUNDS]
        out, bias = refs[2 * ROUNDS :]

        def store(turn, joined):
            for copy in range(XH):
                out[EARLY:, copy, :, turn * HS : (turn + 1) * HS] = joined

        keyvals = [(before[turn], own[turn]) for turn in range(ROUNDS)]
        temporal_scores(clips, place, lengths, queries, keyvals, EARLY, -sources, bias, groups, store)

    return pl.pallas_call(
        body,
        in_specs=[SMEM, SMEM] + [WHOLE] * (1 + 2 * ROUNDS),
        out_specs=WHOLE,
        out_shape=jax.ShapeDtypeStruct((sources, XH, groups * rows, ROUNDS * HS), BF16),
        scratch_shapes=[pltpu.VMEM(((sources - EARLY) * rows, 2 * sources * rows), F32)],
        compiler_params=kernel_params(12),
        cost_estimate=QUICK,
        name="temporal_late",
    )(place, lengths, queries, *own, *before)


def temporal_early(place, lengths, queries, own, before, before2, late, after):
    sources, _, groups, rows, _ = queries.shape
    clips = lengths.shape[0]

    def body(place, lengths, queries, *refs):
        own, before, before2 = (refs[part * ROUNDS : (part + 1) * ROUNDS] for part in range(3))
        out, bias = refs[-2:]

        def store(turn, joined):
            for copy in range(XH):
                out[:, copy, :, turn * HS : (turn + 1) * HS] = joined

        keyvals = [(before2[turn], before[turn], own[turn].at[:EARLY]) for turn in range(ROUNDS)]
        temporal_scores(clips, place, lengths, queries, keyvals, 0, -sources - EARLY, bias, ROUNDS * groups, store)

    block = (EARLY,) + late.shape[1:]
    return pl.pallas_call(
        body,
        grid=(1,),
        in_specs=[SMEM, SMEM] + [WHOLE] * (1 + 3 * ROUNDS) + [ANYWHERE] * 2,
        out_specs=pl.BlockSpec(block, lambda step: (0, 0, 0, 0)),
        out_shape=jax.ShapeDtypeStruct(late.shape, BF16),
        scratch_shapes=[pltpu.VMEM((EARLY * rows, (sources + 2 * EARLY) * rows), F32)],
        input_output_aliases={3 + 3 * ROUNDS: 0},
        compiler_params=kernel_params(12),
        cost_estimate=QUICK,
        name="temporal_early",
    )(place, lengths, queries, *own, *before, *before2, late, after)


def returned_rows(returned, x_half):
    return jnp.concatenate([returned[source, x_half] for source in range(PLANE)], axis=1)


def fetch_rows(sources, starts, targets, arrivals):
    return [
        pltpu.make_async_copy(source.at[pl.ds(start, targets.shape[2])], targets.at[side, part], arrivals.at[side, part])
        for part, start in enumerate(starts)
        for side, source in enumerate(sources)
    ]


def project_first(place, near, far, wo, wo_mate):
    rows, width = near.shape[1:]
    cols = wo.shape[1]

    def body(place, near, far, wo, wo_mate, out, weights, arrivals):
        x_place = place[1]
        starts = [pl.multiple_of(x_place * width, width), pl.multiple_of((1 - x_place) * width, width)]
        copies = fetch_rows((wo, wo_mate), starts, weights, arrivals)
        for copy in copies:
            copy.start()
        lhs = [
            jnp.concatenate([near[0], near[1]], axis=0),
            jnp.concatenate([far[1], far[0]], axis=0),
        ]
        for part in range(2):
            for side in range(2):
                copies[part * 2 + side].wait()
                product = jnp.dot(lhs[part], weights[side, part], preferred_element_type=F32)
                for which in range(2):
                    mine = product[which * rows : (which + 1) * rows]
                    out[which, side] = mine if part == 0 else out[which, side] + mine

    return pl.pallas_call(
        body,
        in_specs=[SMEM] + [WHOLE] * 2 + [IN_HBM] * 2,
        out_specs=WHOLE,
        out_shape=jax.ShapeDtypeStruct((2, 2, rows, cols), F32),
        scratch_shapes=[pltpu.VMEM((2, 2, width, cols), BF16), pltpu.SemaphoreType.DMA((2, 2))],
        compiler_params=kernel_params(LAST_VMEM),
        cost_estimate=QUICK,
        name="project_first",
    )(place, near, far, wo, wo_mate)


def project_last(name, which, place, partial, returned, wo, wo_mate, out_cols, store):
    _, _, rows, cols = partial.shape
    half = wo.shape[0] // 2
    parts = 4
    step = half // parts

    def body(place, partial, returned, wo, wo_mate, out, weights, arrivals):
        copies = fetch_rows((wo, wo_mate), [half + part * step for part in range(parts)], weights, arrivals)
        for copy in copies:
            copy.start()
        left = returned_rows(returned, 1 - place[1] if which else place[1])
        total = [partial[which, 0], partial[which, 1]]
        for part in range(parts):
            for side in range(2):
                copies[part * 2 + side].wait()
                block = left[:, part * step : (part + 1) * step]
                total[side] = total[side] + jnp.dot(block, weights[side, part], preferred_element_type=F32)
        for side in range(2):
            store(place, out, side, total[side].astype(BF16))

    return pl.pallas_call(
        body,
        in_specs=[SMEM] + [WHOLE] * 2 + [IN_HBM] * 2,
        out_specs=WHOLE,
        out_shape=jax.ShapeDtypeStruct((rows, out_cols), BF16),
        scratch_shapes=[pltpu.VMEM((2, parts, step, cols), BF16), pltpu.SemaphoreType.DMA((2, parts))],
        compiler_params=kernel_params(LAST_VMEM),
        cost_estimate=QUICK,
        name=name,
    )(place, partial, returned, wo, wo_mate)


def project_next(place, partial, returned, wo, wo_mate):
    cols = wo.shape[1]

    def store(place, out, side, block):
        out[:, side * cols : (side + 1) * cols] = block

    return project_last("project_next", 1, place, partial, returned, wo, wo_mate, 2 * cols, store)


def project_own(place, partial, returned, wo, wo_mate):
    cols = wo.shape[1]

    def store(place, out, side, block):
        target = place[1] * C + place[2] + side * (1 - 2 * place[2])
        out[:, pl.ds(pl.multiple_of(target * cols, cols), cols)] = block

    return project_last("project_own", 0, place, partial, returned, wo, wo_mate, XH * C * cols, store)


def put_arrived(place, mixed, arrived):
    cols = arrived.shape[1] // 2

    def body(place, mixed, arrived, out, arrivals):
        copies = []
        for side in range(2):
            block = (1 - place[1]) * C + place[2] + side * (1 - 2 * place[2])
            target = out.at[:, pl.ds(pl.multiple_of(block * cols, cols), cols)]
            source = arrived.at[:, side * cols : (side + 1) * cols]
            copies.append(pltpu.make_async_copy(source, target, arrivals.at[side]))
        for copy in copies:
            copy.start()
        for copy in copies:
            copy.wait()

    return pl.pallas_call(
        body,
        in_specs=[SMEM, IN_HBM, ANYWHERE],
        out_specs=IN_HBM,
        out_shape=jax.ShapeDtypeStruct(mixed.shape, mixed.dtype),
        scratch_shapes=[pltpu.SemaphoreType.DMA((2,))],
        input_output_aliases={1: 0},
        compiler_params=kernel_params(4),
        cost_estimate=QUICK,
        name="put_arrived",
    )(place, mixed, arrived)


def on_device(qkv, clip_lengths, wo):
    _, frames, tok, model_width = qkv.shape
    half = model_width // 2
    quarter = half // 2
    x_place = lax.axis_index("xh")
    place = jnp.stack([lax.axis_index("z"), x_place, lax.axis_index("c")]).astype(jnp.int32)

    groups = tok // GROUP
    rows = frames * GROUP

    def by_plane(block, turn):
        split = block.reshape(block.shape[0], frames, groups, GROUP, PLANE, ROUNDS, HS)[:, :, :, :, :, turn]
        return split.transpose(4, 0, 2, 1, 3, 5).reshape(PLANE, -1, groups, rows, HS)

    onward = [(i, (i + 1) % Z) for i in range(Z)]
    queries, last_packed = pack_rest(qkv)
    packed = (by_plane(qkv[1:, :, :, half:], 0), last_packed)
    arrived = [lax.all_to_all(block, ("y", "xl"), 0, 0, tiled=True) for block in packed]

    own_cols = x_place * quarter
    far_cols = (1 - x_place) * quarter
    wo_mate = lax.ppermute(wo, "c", SWAP)
    own = lax.dynamic_slice(qkv, (0, 0, 0, own_cols), (3, frames, tok, quarter))
    far = lax.ppermute(lax.dynamic_slice(qkv, (0, 0, 0, far_cols), (3, frames, tok, quarter)), "xh", SWAP)
    mate_own = lax.ppermute(own, "c", SWAP)
    mate_far = lax.ppermute(far, "c", SWAP)
    near = spatial_attend(own, far, mate_own, mate_far, wo_mate)
    near = near.reshape(2, frames * tok, quarter)
    far = lax.ppermute(near, "xh", SWAP)

    keyvals, before, before2 = [], [], []
    for turn, got in enumerate(arrived):
        if turn:
            got = behind(got, near)
        keyvals.append(got)
        before.append(lax.ppermute(got, "z", onward))
        before2.append(lax.ppermute(before[-1][PLANE - EARLY :], "z", onward))

    queries = lax.all_to_all(queries, ("y", "xl"), 0, 0, tiled=True)
    mine = temporal_late(place, clip_lengths, queries, keyvals, before)
    mine = temporal_early(place, clip_lengths, queries, keyvals, before, before2, mine, far)
    sent = mine.reshape((PLANE * XH,) + mine.shape[2:])
    returned = lax.all_to_all(sent, ("y", "xl", "xh"), 0, 0, tiled=True).reshape(mine.shape)

    partial = project_first(place, near, far, wo, wo_mate)
    for_next = project_next(place, partial, returned, wo, wo_mate)
    arrived = lax.ppermute(for_next, "xh", SWAP)
    mixed = project_own(place, partial, returned, wo, wo_mate)
    return put_arrived(place, mixed, arrived).reshape(frames, tok, model_width)


def solution(mesh):
    fine = Mesh(mesh.devices.reshape(Z, Y, XL, XH, C), ("z", "y", "xl", "xh", "c"))
    return jax.shard_map(
        on_device,
        mesh=fine,
        in_specs=(P(None, ("z", "y", "xl"), ("xh", "c"), None), P(), P(None, ("xh", "c"))),
        out_specs=P(("z", "y", "xl"), ("xh", "c"), None),
        check_vma=False,
    )
```

```python
import jax
import jax.numpy as jnp
import numpy as np
from jax import lax
from jax.experimental import pallas as pl
from jax.experimental.pallas import tpu as pltpu
from jax.sharding import Mesh, PartitionSpec as P

HS = 128
Z, Y, XL, XH, C = 8, 4, 2, 2, 2
PLANE = Y * XL
EXP2_SCALE = HS ** (-0.5) * float(np.log2(np.e))
F32 = jnp.float32
BF16 = jnp.bfloat16
GROUP = 8
ROUNDS = 2

SWAP = [(0, 1), (1, 0)]

SMEM = pl.BlockSpec(memory_space=pltpu.SMEM)
WHOLE = pl.BlockSpec(memory_space=pltpu.VMEM)
ANYWHERE = pl.BlockSpec(memory_space=pl.ANY)
IN_HBM = pl.BlockSpec(memory_space=pltpu.HBM)
PACK_VMEM = 60
LAST_VMEM = 44
QUICK = pl.CostEstimate(flops=1024, bytes_accessed=1024, transcendentals=0)


def kernel_params(mebibytes):
    return pltpu.CompilerParams(vmem_limit_bytes=mebibytes * 1024 * 1024)


def behind(array, *after):
    def body(*refs):
        pass

    return pl.pallas_call(
        body,
        in_specs=[ANYWHERE] * (1 + len(after)),
        out_specs=ANYWHERE,
        out_shape=jax.ShapeDtypeStruct(array.shape, array.dtype),
        input_output_aliases={0: 0},
        compiler_params=kernel_params(1),
        cost_estimate=QUICK,
        name="behind",
    )(array, *after)


def softmax_parts(scores):
    top = jnp.max(scores, axis=-1, keepdims=True)
    return jnp.exp2((scores - top) * EXP2_SCALE).astype(BF16)


def weighted(raised, values):
    both = jnp.concatenate([values, jnp.ones_like(values)], axis=1)
    result = jnp.dot(raised, both, preferred_element_type=F32)
    return result[:, :HS] / result[:, HS:]


def pack(qkv):
    _, frames, tok, model_width = qkv.shape
    half = model_width // 2
    groups = tok // GROUP
    step = 2
    contents = [[(0, turn) for turn in range(ROUNDS)]] + [[(1, turn), (2, turn)] for turn in range(ROUNDS)]

    def body(qkv, *outs):
        for out, slots in zip(outs, contents):
            for device in range(PLANE):
                for slot, (which, turn) in enumerate(slots):
                    first = (device * ROUNDS + turn) * HS
                    block = qkv[which, :, :, first : first + HS].astype(F32).reshape(step, groups, GROUP, HS)
                    for group in range(groups):
                        out[device, slot, group] = block[:, group].reshape(step * GROUP, HS).astype(BF16)

    rows = jax.ShapeDtypeStruct((PLANE, 2, groups, frames * GROUP, HS), BF16)
    rows_spec = pl.BlockSpec((PLANE, 2, groups, step * GROUP, HS), lambda f: (0, 0, 0, f, 0))
    return pl.pallas_call(
        body,
        grid=(frames // step,),
        in_specs=[pl.BlockSpec((3, step, tok, half), lambda f: (0, f, 0, 1))],
        out_specs=[rows_spec] * len(contents),
        out_shape=[rows] * len(contents),
        compiler_params=kernel_params(PACK_VMEM),
        cost_estimate=QUICK,
        name="pack",
    )(qkv)


def spatial_attend(own, queries_far, keyvals_far, mate_own, mate_far, after):
    _, frames, tok, width = own.shape

    def body(own, queries_far, keyvals_far, mate_own, mate_far, after, out):
        blocks = [(f, slice(head * HS, (head + 1) * HS)) for f in range(frames) for head in range(width // HS)]

        def keyvals_of(which, f, cols):
            parts = ((own, 1), (keyvals_far, 0), (mate_own, 1), (mate_far, 0))
            return jnp.concatenate([ref[skip + which, f, :, cols] for ref, skip in parts], axis=0)

        for first in range(0, len(blocks), 8):
            batch = blocks[first : first + 8]
            scores = []
            for f, cols in batch:
                queries = jnp.concatenate([own[0, f, :, cols], queries_far[0, f, :, cols]], axis=0)
                scores.append(
                    lax.dot_general(
                        queries, keyvals_of(0, f, cols), (((1,), (1,)), ((), ())), preferred_element_type=F32
                    )
                )
            raised = [softmax_parts(block) for block in scores]
            results = [weighted(block, keyvals_of(1, f, cols)).astype(BF16) for block, (f, cols) in zip(raised, batch)]
            for result, (f, cols) in zip(results, batch):
                out[0, f, :, cols] = result[:tok]
                out[1, f, :, cols] = result[tok:]

    return pl.pallas_call(
        body,
        in_specs=[WHOLE] * 5 + [ANYWHERE],
        out_specs=WHOLE,
        out_shape=jax.ShapeDtypeStruct((2, frames, tok, width), BF16),
        compiler_params=kernel_params(16),
        cost_estimate=QUICK,
        name="spatial",
    )(own, queries_far, keyvals_far, mate_own, mate_far, after)


def temporal_scores(clips, place, lengths, queries, keyvals, first_query, first_key, bias, batch, store):
    _, _, groups, rows, _ = queries.shape
    frames_dev = rows // GROUP
    query_rows, key_count = bias.shape
    first = place[0] * (PLANE * frames_dev)

    row = lax.broadcasted_iota(jnp.int32, (query_rows, 1), 0)
    frame = first + first_query * frames_dev + row // GROUP
    start = jnp.zeros_like(frame)
    begin = jnp.int32(0)
    for clip in range(clips):
        start = jnp.where(frame >= begin, begin, start)
        begin = begin + lengths[clip]
    oldest = first + first_key * frames_dev
    token = (row % GROUP) * 4096
    low = token + start - oldest
    high = token + frame - oldest
    col = lax.broadcasted_iota(jnp.int32, (1, key_count), 1)
    code = (col % GROUP) * 4096 + col // GROUP
    bias[...] = jnp.where((code >= low) & (code <= high), 0.0, -1e30)

    blocks = slice(first_query, first_query + query_rows // rows)
    def rows_of(which, turn, group):
        return jnp.concatenate([part[:, which, group].reshape(-1, HS) for part in keyvals[turn]], axis=0)

    units = [(turn, group) for turn in range(ROUNDS) for group in range(groups)]
    for first_unit in range(0, len(units), batch):
        some = units[first_unit : first_unit + batch]
        scores = [
            lax.dot_general(
                queries[blocks, turn, group].reshape(-1, HS),
                rows_of(0, turn, group),
                (((1,), (1,)), ((), ())),
                preferred_element_type=F32,
            )
            for turn, group in some
        ]
        raised = [softmax_parts(block + bias[...]) for block in scores]
        results = [weighted(block, rows_of(1, turn, group)) for block, (turn, group) in zip(raised, some)]
        for at in range(0, len(some), groups):
            pieces = [result.reshape(-1, 1, GROUP, HS) for result in results[at : at + groups]]
            joined = jnp.concatenate(pieces, axis=1).reshape(-1, frames_dev * groups * GROUP, HS).astype(BF16)
            store(some[at][0], joined)


EARLY = 2


def temporal_late(place, lengths, queries, own, before):
    sources, _, groups, rows, _ = queries.shape
    clips = lengths.shape[0]

    def body(place, lengths, queries, *refs):
        own, before = refs[:ROUNDS], refs[ROUNDS : 2 * ROUNDS]
        out, bias = refs[2 * ROUNDS :]

        def store(turn, joined):
            for copy in range(XH):
                out[EARLY:, copy, :, turn * HS : (turn + 1) * HS] = joined

        keyvals = [(before[turn], own[turn]) for turn in range(ROUNDS)]
        temporal_scores(clips, place, lengths, queries, keyvals, EARLY, -sources, bias, groups, store)

    return pl.pallas_call(
        body,
        in_specs=[SMEM, SMEM] + [WHOLE] * (1 + 2 * ROUNDS),
        out_specs=WHOLE,
        out_shape=jax.ShapeDtypeStruct((sources, XH, groups * rows, ROUNDS * HS), BF16),
        scratch_shapes=[pltpu.VMEM(((sources - EARLY) * rows, 2 * sources * rows), F32)],
        compiler_params=kernel_params(12),
        cost_estimate=QUICK,
        name="temporal_late",
    )(place, lengths, queries, *own, *before)


def temporal_early(place, lengths, queries, own, before, before2, late, after):
    sources, _, groups, rows, _ = queries.shape
    clips = lengths.shape[0]

    def body(place, lengths, queries, *refs):
        own, before, before2 = (refs[part * ROUNDS : (part + 1) * ROUNDS] for part in range(3))
        out, bias = refs[-2:]

        def store(turn, joined):
            for copy in range(XH):
                out[:, copy, :, turn * HS : (turn + 1) * HS] = joined

        keyvals = [(before2[turn], before[turn], own[turn].at[:EARLY]) for turn in range(ROUNDS)]
        temporal_scores(clips, place, lengths, queries, keyvals, 0, -sources - EARLY, bias, ROUNDS * groups, store)

    block = (EARLY,) + late.shape[1:]
    return pl.pallas_call(
        body,
        grid=(1,),
        in_specs=[SMEM, SMEM] + [WHOLE] * (1 + 3 * ROUNDS) + [ANYWHERE] * 2,
        out_specs=pl.BlockSpec(block, lambda step: (0, 0, 0, 0)),
        out_shape=jax.ShapeDtypeStruct(late.shape, BF16),
        scratch_shapes=[pltpu.VMEM((EARLY * rows, (sources + 2 * EARLY) * rows), F32)],
        input_output_aliases={3 + 3 * ROUNDS: 0},
        compiler_params=kernel_params(12),
        cost_estimate=QUICK,
        name="temporal_early",
    )(place, lengths, queries, *own, *before, *before2, late, after)


def returned_rows(returned, x_half):
    return jnp.concatenate([returned[source, x_half] for source in range(PLANE)], axis=1)


def fetch_rows(sources, starts, targets, arrivals):
    return [
        pltpu.make_async_copy(source.at[pl.ds(start, targets.shape[2])], targets.at[side, part], arrivals.at[side, part])
        for part, start in enumerate(starts)
        for side, source in enumerate(sources)
    ]


def project_first(place, near, far, wo, wo_mate):
    rows, width = near.shape[1:]
    cols = wo.shape[1]

    def body(place, near, far, wo, wo_mate, out, weights, arrivals):
        x_place = place[1]
        starts = [pl.multiple_of(x_place * width, width), pl.multiple_of((1 - x_place) * width, width)]
        copies = fetch_rows((wo, wo_mate), starts, weights, arrivals)
        for copy in copies:
            copy.start()
        lhs = [
            jnp.concatenate([near[0], near[1]], axis=0),
            jnp.concatenate([far[1], far[0]], axis=0),
        ]
        for part in range(2):
            for side in range(2):
                copies[part * 2 + side].wait()
                product = jnp.dot(lhs[part], weights[side, part], preferred_element_type=F32)
                for which in range(2):
                    mine = product[which * rows : (which + 1) * rows]
                    out[which, side] = mine if part == 0 else out[which, side] + mine

    return pl.pallas_call(
        body,
        in_specs=[SMEM] + [WHOLE] * 2 + [IN_HBM] * 2,
        out_specs=WHOLE,
        out_shape=jax.ShapeDtypeStruct((2, 2, rows, cols), F32),
        scratch_shapes=[pltpu.VMEM((2, 2, width, cols), BF16), pltpu.SemaphoreType.DMA((2, 2))],
        compiler_params=kernel_params(LAST_VMEM),
        cost_estimate=QUICK,
        name="project_first",
    )(place, near, far, wo, wo_mate)


def project_last(name, which, place, partial, returned, wo, wo_mate, out_cols, store):
    _, _, rows, cols = partial.shape
    half = wo.shape[0] // 2
    parts = 4
    step = half // parts

    def body(place, partial, returned, wo, wo_mate, out, weights, arrivals):
        copies = fetch_rows((wo, wo_mate), [half + part * step for part in range(parts)], weights, arrivals)
        for copy in copies:
            copy.start()
        left = returned_rows(returned, 1 - place[1] if which else place[1])
        total = [partial[which, 0], partial[which, 1]]
        for part in range(parts):
            for side in range(2):
                copies[part * 2 + side].wait()
                block = left[:, part * step : (part + 1) * step]
                total[side] = total[side] + jnp.dot(block, weights[side, part], preferred_element_type=F32)
        for side in range(2):
            store(place, out, side, total[side].astype(BF16))

    return pl.pallas_call(
        body,
        in_specs=[SMEM] + [WHOLE] * 2 + [IN_HBM] * 2,
        out_specs=WHOLE,
        out_shape=jax.ShapeDtypeStruct((rows, out_cols), BF16),
        scratch_shapes=[pltpu.VMEM((2, parts, step, cols), BF16), pltpu.SemaphoreType.DMA((2, parts))],
        compiler_params=kernel_params(LAST_VMEM),
        cost_estimate=QUICK,
        name=name,
    )(place, partial, returned, wo, wo_mate)


def project_next(place, partial, returned, wo, wo_mate):
    cols = wo.shape[1]

    def store(place, out, side, block):
        out[:, side * cols : (side + 1) * cols] = block

    return project_last("project_next", 1, place, partial, returned, wo, wo_mate, 2 * cols, store)


def project_own(place, partial, returned, wo, wo_mate):
    cols = wo.shape[1]

    def store(place, out, side, block):
        target = place[1] * C + place[2] + side * (1 - 2 * place[2])
        out[:, pl.ds(pl.multiple_of(target * cols, cols), cols)] = block

    return project_last("project_own", 0, place, partial, returned, wo, wo_mate, XH * C * cols, store)


def put_arrived(place, mixed, arrived):
    rows, width = arrived.shape
    cols = width // 2

    def body(place, mixed, arrived, out):
        out[...] = arrived[...]

    def target(side, place):
        return 0, (1 - place[1]) * C + place[2] + side * (1 - 2 * place[2])

    return pl.pallas_call(
        body,
        grid_spec=pltpu.PrefetchScalarGridSpec(
            num_scalar_prefetch=1,
            grid=(2,),
            in_specs=[ANYWHERE, pl.BlockSpec((rows, cols), lambda side, place: (0, side))],
            out_specs=pl.BlockSpec((rows, cols), target),
        ),
        out_shape=jax.ShapeDtypeStruct(mixed.shape, mixed.dtype),
        input_output_aliases={1: 0},
        compiler_params=kernel_params(16),
        cost_estimate=QUICK,
        name="put_arrived",
    )(place, mixed, arrived)


def on_device(qkv, clip_lengths, wo):
    _, frames, tok, model_width = qkv.shape
    quarter = model_width // 4
    x_place = lax.axis_index("xh")
    place = jnp.stack([lax.axis_index("z"), x_place, lax.axis_index("c")]).astype(jnp.int32)

    onward = [(i, (i + 1) % Z) for i in range(Z)]
    queries, *packed = pack(qkv)
    arrived = [lax.all_to_all(block, ("y", "xl"), 0, 0, tiled=True) for block in packed]

    own_cols = x_place * quarter
    far_cols = (1 - x_place) * quarter
    wo_mate = lax.ppermute(wo, "c", SWAP)
    own = lax.dynamic_slice(qkv, (0, 0, 0, own_cols), (3, frames, tok, quarter))
    keyvals_far = lax.dynamic_slice(qkv, (1, 0, 0, far_cols), (2, frames, tok, quarter))
    keyvals_far = lax.ppermute(keyvals_far, "xh", SWAP)
    queries_far = lax.dynamic_slice(qkv, (0, 0, 0, far_cols), (1, frames, tok, quarter))
    queries_far = lax.ppermute(behind(queries_far, keyvals_far), "xh", SWAP)
    mate_own = lax.ppermute(own, "c", SWAP)
    mate_far = lax.ppermute(keyvals_far, "c", SWAP)
    near = spatial_attend(own, queries_far, keyvals_far, mate_own, mate_far, wo_mate)
    near = near.reshape(2, frames * tok, quarter)
    far = lax.ppermute(near, "xh", SWAP)

    keyvals, before, before2 = [], [], []
    for turn, got in enumerate(arrived):
        if turn:
            got = behind(got, near)
        keyvals.append(got)
        before.append(lax.ppermute(got, "z", onward))
        before2.append(lax.ppermute(before[-1][PLANE - EARLY :], "z", onward))

    queries = lax.all_to_all(queries, ("y", "xl"), 0, 0, tiled=True)
    mine = temporal_late(place, clip_lengths, queries, keyvals, before)
    mine = temporal_early(place, clip_lengths, queries, keyvals, before, before2, mine, far)
    sent = mine.reshape((PLANE * XH,) + mine.shape[2:])
    returned = lax.all_to_all(sent, ("y", "xl", "xh"), 0, 0, tiled=True).reshape(mine.shape)

    partial = project_first(place, near, far, wo, wo_mate)
    for_next = project_next(place, partial, returned, wo, wo_mate)
    arrived = lax.ppermute(for_next, "xh", SWAP)
    mixed = project_own(place, partial, returned, wo, wo_mate)
    return put_arrived(place, mixed, arrived).reshape(frames, tok, model_width)


def solution(mesh):
    fine = Mesh(mesh.devices.reshape(Z, Y, XL, XH, C), ("z", "y", "xl", "xh", "c"))
    return jax.shard_map(
        on_device,
        mesh=fine,
        in_specs=(P(None, ("z", "y", "xl"), ("xh", "c"), None), P(), P(None, ("xh", "c"))),
        out_specs=P(("z", "y", "xl"), ("xh", "c"), None),
        check_vma=False,
    )
```
